512 devices in a mesh: run: 16 (over z_lo, y), tile: 32 (over x, z_hi, core).
Axes of the slice: x: 4, y: 8, z: 8 (z_hi: 4, z_lo: 2; z = z_hi * 2 + z_lo), core: 2. Of those that a mesh axis runs over, the one named last changes fastest.
Arguments:
- state: float32 [16, 5, 8, 256, 128], P('run', None, None, 'tile'), as said below
- spacing_index: int32 [16], P('run'), may hold values from 1 to 3
- strength_index: int32 [16], P('run'), may hold values from 0 to 3
- obs_offsets: int32 [8, 2], replicated, may hold values from 0 to 1
Outputs:
- final_state: float32 [16, 5, 8, 256, 128], P('run', None, None, 'tile')
- misfit: float32 [16], P('run')
The draws below stay inside these ranges and needn't reach their ends.
Inputs may be any that keep to these rules, and one draw needn't show every extreme that they name: `state`: components 0 and 4 (density and temperature) lie between 0.8 and 1.2; velocities are of order 0.1.
All inputs are finite; a program needn't handle non-finite values.
Results may differ from the reference program's by a relative error of at most 0.0003.
Values sent between devices are 32-bit elements; how exact they have to be, the bound alone decides.
No kernel may reach another device: no remote copies, remote signals or barrier semaphores. Data moves between devices by JAX's collectives and lax.ppermute only.
A program may use at most 64 MiB of HBM per device.

```python
import jax
import jax.numpy as jnp
from jax import lax

LATTICE_SITES_N = 128
LAYER_NUMBER = 8
STEPS = 3
MEMBER_TOTAL = 16
LATTICE_SITES_E = 256


def draw_state(key, part):
    random_seed_rho, random_seed_motion, random_seed_warmth = jax.random.split(key, 3)
    matter_per_volume = jax.random.uniform(random_seed_rho, (MEMBER_TOTAL, 1, LAYER_NUMBER, LATTICE_SITES_E, LATTICE_SITES_N), jnp.float32, 0.8, 1.2)
    stream_speed_vector = 0.1 * jax.random.normal(random_seed_motion, (MEMBER_TOTAL, 3, LAYER_NUMBER, LATTICE_SITES_E, LATTICE_SITES_N), jnp.float32)
    warmth_field = jax.random.uniform(random_seed_warmth, (MEMBER_TOTAL, 1, LAYER_NUMBER, LATTICE_SITES_E, LATTICE_SITES_N), jnp.float32, 0.8, 1.2)
    return jnp.concatenate([matter_per_volume, stream_speed_vector, warmth_field], axis=1)


def touch_ends(drawn, stream_key, smallest, high):
    longest = drawn.shape.index(max(drawn.shape))
    spots = []
    for shift in (0, 1):
        where = [jax.random.randint(jax.random.fold_in(stream_key, axis), (), 0, length) for axis, length in enumerate(drawn.shape)]
        where[longest] = (where[longest] + shift) % drawn.shape[longest]
        spots.append(tuple(where))
    return drawn.at[spots[0]].set(smallest).at[spots[1]].set(high)


def setup_inputs(seed: int = 0) -> dict:
    key_list = jax.random.split(jax.random.key(seed), 5)
    return {
        "state": draw_state(jax.random.fold_in(key_list[4], 71), 0),
        "spacing_index": touch_ends(jax.random.randint(key_list[1], (MEMBER_TOTAL,), 1, 4), jax.random.fold_in(key_list[1], 1), 1, 3).astype(jnp.int32),
        "strength_index": touch_ends(jax.random.randint(key_list[2], (MEMBER_TOTAL,), 0, 4), jax.random.fold_in(key_list[2], 1), 0, 3).astype(jnp.int32),
        "obs_offsets": touch_ends(jax.random.randint(key_list[3], (LAYER_NUMBER, 2), 0, 2), jax.random.fold_in(key_list[3], 1), 0, 1).astype(jnp.int32),
    }


time_step = 0.05
viscosity = 0.05
conduction_coefficient = 0.05
adiabatic_index = 1.4
gravity = 0.5
hot_wall = 1.2
cold_wall = 0.8


def pad_vertical(fields):
    signs = jnp.array([1.0, 1.0, 1.0, -1.0, -1.0], jnp.float32).reshape(5, 1, 1, 1)
    bottom_add = jnp.array([0.0, 0.0, 0.0, 0.0, 2.0 * hot_wall], jnp.float32).reshape(5, 1, 1, 1)
    top_add = jnp.array([0.0, 0.0, 0.0, 0.0, 2.0 * cold_wall], jnp.float32).reshape(5, 1, 1, 1)
    bottom = signs * fields[:, :1] + bottom_add
    top = signs * fields[:, -1:] + top_add
    return jnp.concatenate([bottom, fields, top], axis=1)


def inner_domain(values):
    return values[..., 1:-1, 1:-1, :]


def deriv_x(values):
    return 0.5 * (values[..., 1:-1, 2:, :] - values[..., 1:-1, :-2, :])


def deriv_y(values):
    centre = inner_domain(values)
    return 0.5 * (jnp.roll(centre, -1, -1) - jnp.roll(centre, 1, -1))


def deriv_z(values):
    return 0.5 * (values[..., 2:, 1:-1, :] - values[..., :-2, 1:-1, :])


def second_derivative_sum(values):
    centre = inner_domain(values)
    total = values[..., 2:, 1:-1, :] + values[..., :-2, 1:-1, :]
    total = total + values[..., 1:-1, 2:, :] + values[..., 1:-1, :-2, :]
    total = total + jnp.roll(centre, -1, -1) + jnp.roll(centre, 1, -1)
    return total - 6.0 * centre


def tendency(xpadded):
    device_arrangement = pad_vertical(xpadded)
    matter_per_volume = device_arrangement[0]
    stream_speed_vector = device_arrangement[1:4]
    warmth_field = device_arrangement[4]
    mass_flux = deriv_x(matter_per_volume * device_arrangement[1]) + deriv_y(matter_per_volume * device_arrangement[2]) + deriv_z(matter_per_volume * device_arrangement[3])
    normal_stress_field = matter_per_volume * warmth_field
    centre_vel = inner_domain(stream_speed_vector)
    centre_den = inner_domain(matter_per_volume)
    middle_warmth_value = inner_domain(warmth_field)

    def transport_contribution(quantity):
        return centre_vel[0] * deriv_x(quantity) + centre_vel[1] * deriv_y(quantity) + centre_vel[2] * deriv_z(quantity)

    gradient = jnp.stack([deriv_x(normal_stress_field), deriv_y(normal_stress_field), deriv_z(normal_stress_field)])
    lift = jnp.array([0.0, 0.0, gravity], jnp.float32).reshape(3, 1, 1, 1)
    accel = -transport_contribution(stream_speed_vector) - gradient / centre_den + viscosity * second_derivative_sum(stream_speed_vector) - lift
    outflow_spread = deriv_x(device_arrangement[1]) + deriv_y(device_arrangement[2]) + deriv_z(device_arrangement[3])
    internal_warming = -transport_contribution(warmth_field) - (adiabatic_index - 1.0) * middle_warmth_value * outflow_spread + conduction_coefficient * second_derivative_sum(warmth_field)
    return jnp.concatenate([-mass_flux[None], accel, internal_warming[None]], axis=0)


def reference(state, spacing_index, strength_index, obs_offsets):
    offset_x = obs_offsets[:, 0].astype(jnp.int32)
    offset_y = obs_offsets[:, 1].astype(jnp.int32)
    cells_x = jnp.arange(LATTICE_SITES_E, dtype=jnp.int32)
    cells_y = jnp.arange(LATTICE_SITES_N, dtype=jnp.int32)
    run_ids = jnp.arange(MEMBER_TOTAL, dtype=jnp.int32)
    strengths = jnp.where(run_ids == 0, 0.0, 0.5 * jnp.exp2(strength_index.astype(jnp.float32))).astype(jnp.float32)
    spacings = jnp.left_shift(jnp.ones_like(spacing_index), spacing_index).astype(jnp.int32)
    misfit = jnp.zeros((MEMBER_TOTAL,), jnp.float32)
    for iteration in range(STEPS):
        nature = state[0, 1:5]

        def advance(item):
            fields, strength, spacing = item
            index_x = ((cells_x[None, :] // spacing) * spacing + offset_x[:, None]).astype(jnp.int32)
            index_y = ((cells_y[None, :] // spacing) * spacing + offset_y[:, None]).astype(jnp.int32)
            gap = fields[1:5] - nature
            full_x = jnp.broadcast_to(index_x[None, :, :, None], gap.shape).astype(jnp.int32)
            picked = jnp.take_along_axis(gap, full_x, axis=2)
            full_y = jnp.broadcast_to(index_y[None, :, None, :], gap.shape).astype(jnp.int32)
            observed = jnp.take_along_axis(picked, full_y, axis=3)
            xpadded = jnp.concatenate([fields[:, :, -1:], fields, fields[:, :, :1]], axis=2)
            nudged = tendency(xpadded) - strength * jnp.pad(observed, ((1, 0), (0, 0), (0, 0), (0, 0)))
            updated = fields + time_step * nudged
            return updated, jnp.mean(observed[3] * observed[3])

        state, misfit = lax.map(advance, (state, strengths, spacings))
    return state, misfit
```

```python
import jax
import jax.numpy as jnp
from jax import lax
from jax.experimental import pallas as pl
from jax.experimental.pallas import tpu as pltpu
from jax.sharding import PartitionSpec as P

RUNS = 16
TILES = 32
PLANES = 8
CELLS = 8 * 256 * 128

DT = 0.05
VISC = 0.05
GAMMA1 = 0.4
GRAVITY = 0.5
HOT = 1.2
COLD = 0.8

ROWS = (8, 128)


def rolled(v, shift, axis):
    return pltpu.roll(v, shift % v.shape[axis], axis)


def sub_ids():
    return lax.broadcasted_iota(jnp.int32, ROWS, 0)


def lane_ids():
    return lax.broadcasted_iota(jnp.int32, ROWS, 1)


class Spread:
    def __init__(self, sp_ref, off_ref):
        sub, lane = sub_ids(), lane_ids()
        k = sp_ref[0]
        self.off = off_ref
        self.sub_odd = (sub & 1) == 1
        self.lane_odd = (lane & 1) == 1
        self.masks = []
        for ids in (sub, lane):
            self.masks.append(
                tuple(((ids & bit) != 0) & (k >= level) for bit, level in ((2, 2), (4, 3)))
            )
        self.sub1, self.lane1 = sub & 1, lane & 1

    def plane(self, z):
        return self.sub1 == self.off[z, 0], self.lane1 == self.off[z, 1]

    def __call__(self, e, keep):
        for axis in (0, 1):
            odd = (self.sub_odd, self.lane_odd)[axis]
            swapped = jnp.where(odd, rolled(e, 1, axis), rolled(e, -1, axis))
            e = jnp.where(keep[axis], e, swapped)
            for mask, shift in zip(self.masks[axis], (2, 4)):
                e = jnp.where(mask, rolled(e, shift, axis), e)
        return e


def ghosted(load):
    def get(c, z, t):
        if z < 0:
            edge = load(c, 0, t)
            return edge if c < 3 else -edge if c == 3 else 2.0 * HOT - edge
        if z >= PLANES:
            edge = load(c, PLANES - 1, t)
            return edge if c < 3 else -edge if c == 3 else 2.0 * COLD - edge
        return load(c, z, t)

    return get


def neighbours_x(a, b, sub):
    a1, b1 = rolled(a, -1, 0), rolled(b, -1, 0)
    a2, b2 = rolled(a, 1, 0), rolled(b, 1, 0)
    last, first = sub == 7, sub == 0
    return (
        (jnp.where(last, b1, a1), jnp.where(last, a1, b1)),
        (jnp.where(first, b2, a2), jnp.where(first, a2, b2)),
    )


def stepped(get, z, tiles, sub):
    centre = [[get(c, z, t) for t in (0, 1)] for c in range(5)]
    along_x = [neighbours_x(v[0], v[1], sub) for v in centre]
    result = []
    for t in tiles:
        c0 = [v[t] for v in centre]
        xn = [v[0][t] for v in along_x]
        xp = [v[1][t] for v in along_x]
        yn = [rolled(v, -1, 1) for v in c0]
        yp = [rolled(v, 1, 1) for v in c0]
        zn = [get(c, z + 1, t) for c in range(5)]
        zp = [get(c, z - 1, t) for c in range(5)]
        flux = (
            (xn[0] * xn[1] - xp[0] * xp[1])
            + (yn[0] * yn[2] - yp[0] * yp[2])
            + (zn[0] * zn[3] - zp[0] * zp[3])
        )
        scale = (0.5 * DT) / c0[0]
        grad = (
            xn[0] * xn[4] - xp[0] * xp[4],
            yn[0] * yn[4] - yp[0] * yp[4],
            zn[0] * zn[4] - zp[0] * zp[4],
        )
        new = [c0[0] - (0.5 * DT) * flux]
        div = None
        for q in range(1, 5):
            dx, dy, dz = xn[q] - xp[q], yn[q] - yp[q], zn[q] - zp[q]
            part = (None, dx, dy, dz, None)[q]
            if part is not None:
                div = part if div is None else div + part
            adv = c0[1] * dx + c0[2] * dy + c0[3] * dz
            six = ((xn[q] + xp[q]) + (yn[q] + yp[q])) + (zn[q] + zp[q])
            change = (DT * VISC) * (six - 6.0 * c0[q]) - (0.5 * DT) * adv
            if q < 4:
                change = change - grad[q - 1] * scale
                if q == 3:
                    change = change - DT * GRAVITY
            else:
                change = change - (0.5 * DT * GAMMA1) * (c0[4] * div)
            new.append(c0[q] + change)
        result.append(new)
    return result


def nudge_factor(st_ref):
    strength = 0.5 * lax.shift_left(jnp.int32(1), st_ref[0]).astype(jnp.float32)
    return jnp.where(lax.axis_index("run") == 0, 0.0, DT * strength)


def pack_kernel(sp_ref, off_ref, own_ref, y_ref, p_ref, q_ref, nat_ref, d_ref, near_ref, far_ref):
    spread = Spread(sp_ref, off_ref)
    sub = sub_ids()
    even = lax.rem(lax.axis_index("tile"), 2) == 0
    to_near = (sub >= 4) == even
    for z in range(PLANES):
        keep = spread.plane(z)
        for c in range(5):
            own = own_ref[c, z]
            nat = y_ref[c, z] + p_ref[c, z] + q_ref[c, z]
            nat_ref[c, z] = nat
            if c > 0:
                d = spread(own - nat, keep)
                d_ref[c - 1, z] = d
                own = jnp.where(sub == 5, rolled(d, -2, 0), own)
            other = rolled(nat, 4, 0)
            near_ref[c, z] = jnp.where(to_near, own, other)
            far_ref[c, z] = jnp.where(to_near, other, own)


def steps_kernel(
    sp_ref, st_ref, off_ref, own_ref, nat_ref, d_ref, near_ref, far_ref,
    own2_ref, beyond_ref, edge_ref, d2_ref, sum_ref, a_ref, b_ref, a1_ref, b1_ref, n2_ref,
):
    spread = Spread(sp_ref, off_ref)
    sub = sub_ids()
    even = lax.rem(lax.axis_index("tile"), 2) == 0
    from_near = (sub < 4) == even
    mu = nudge_factor(st_ref)
    for c in range(5):
        for z in range(PLANES):
            near, far = near_ref[c, z], far_ref[c, z]
            a_ref[c, z] = jnp.where(from_near, near, far)
            b_ref[c, z] = rolled(jnp.where(from_near, far, near), 4, 0)
    a = ghosted(lambda c, z, t: a_ref[c, z] if t else own_ref[c, z])
    b = ghosted(lambda c, z, t: b_ref[c, z] if t else nat_ref[c, z])
    for z in range(PLANES):
        keep = spread.plane(z)
        new_a = stepped(a, z, (0, 1), sub)
        new_b = stepped(b, z, (0, 1), sub)
        for t in (0, 1):
            for c in range(5):
                value = new_a[t][c]
                if c > 0:
                    if t == 0:
                        d = d_ref[c - 1, z]
                    else:
                        halo = a_ref[c, z]
                        d = spread(halo - b_ref[c, z], keep)
                        d = jnp.where(sub == 7, rolled(halo, 2, 0), d)
                    value = value - mu * d
                a1_ref[t, c, z] = value
                b1_ref[t, c, z] = new_b[t][c]
    a = ghosted(lambda c, z, t: a1_ref[t, c, z])
    b = ghosted(lambda c, z, t: b1_ref[t, c, z])
    total = jnp.zeros(ROWS, jnp.float32)
    for z in range(PLANES):
        keep = spread.plane(z)
        new_a = stepped(a, z, (0, 1), sub)
        new_b = stepped(b, z, (0,), sub)[0]
        for c in range(5):
            for t in (0, 1):
                value = new_a[t][c]
                if c > 0:
                    value = value - mu * spread(a1_ref[t, c, z] - b1_ref[t, c, z], keep)
                if t == 0:
                    own2_ref[c, z] = value
                    edge_ref[c, z : z + 1] = value[7:8]
                    if c > 0:
                        d = spread(value - new_b[c], keep)
                        d2_ref[c - 1, z] = d
                        if c == 4:
                            total = total + d * d
                else:
                    beyond_ref[c, z : z + 1] = value[0:1]
    sum_ref[...] = jnp.broadcast_to(jnp.sum(total, axis=0)[None, None], sum_ref.shape)


def last_kernel(st_ref, own_ref, beyond_ref, edge_ref, d_ref, sums_ref, out_ref, misfit_ref, h_ref):
    sub = sub_ids()
    mu = nudge_factor(st_ref)
    for c in range(5):
        for z in range(PLANES):
            h_ref[c, z] = jnp.where(
                sub == 0,
                jnp.broadcast_to(beyond_ref[c, z : z + 1], ROWS),
                jnp.broadcast_to(edge_ref[c, z : z + 1], ROWS),
            )
    a = ghosted(lambda c, z, t: h_ref[c, z] if t else own_ref[c, z])
    for z in range(PLANES):
        new = stepped(a, z, (0,), sub)[0]
        for c in range(5):
            value = new[c]
            if c > 0:
                value = value - mu * d_ref[c - 1, z]
            out_ref[c, z] = value
    misfit_ref[0] = jnp.sum(sums_ref[...]) * (1.0 / CELLS)


def f32(*shape):
    return jax.ShapeDtypeStruct(shape, jnp.float32)


VM = pl.BlockSpec(memory_space=pltpu.VMEM)
SM = pl.BlockSpec(memory_space=pltpu.SMEM)
PARAMS = pltpu.CompilerParams(vmem_limit_bytes=12 * 2**20)
BLOCK = (5, PLANES, 8, 128)
BLOCK4 = (4, PLANES, 8, 128)


def twice(pairs):
    return pairs + [(a + 8, b + 8) for a, b in pairs]


def shards(state, spacing_index, strength_index, obs_offsets):
    own = state[0]
    run = lax.axis_index("run")

    p = lax.ppermute(own, "run", [(0, 8)])
    y = jnp.where(run == 0, own, p)
    p = lax.ppermute(y, "run", twice([(0, 3)]))
    q = lax.ppermute(y, "run", twice([(0, 5)]))
    y = y + p + q
    p = lax.ppermute(y, "run", twice([(0, 1), (3, 4), (5, 6)]))
    q = lax.ppermute(y, "run", twice([(0, 7), (3, 2)]))

    nat, d, near, far = pl.pallas_call(
        pack_kernel,
        out_shape=(f32(*BLOCK), f32(*BLOCK4), f32(*BLOCK), f32(*BLOCK)),
        in_specs=[SM, SM, VM, VM, VM, VM],
        out_specs=(VM,) * 4,
        compiler_params=PARAMS,
        name="pack",
    )(spacing_index, obs_offsets, own, y, p, q)

    far = lax.ppermute(
        far, "tile", [(i, (i + 1) % TILES if i % 2 else (i - 1) % TILES) for i in range(TILES)]
    )
    near = lax.ppermute(near, "tile", [(i, i ^ 1) for i in range(TILES)])

    own2, beyond, edge, d2, sums = pl.pallas_call(
        steps_kernel,
        out_shape=(
            f32(*BLOCK), f32(5, PLANES, 128), f32(5, PLANES, 128), f32(*BLOCK4), f32(TILES, 1, 128)
        ),
        in_specs=[SM, SM, SM] + [VM] * 5,
        out_specs=(VM,) * 5,
        scratch_shapes=[
            pltpu.VMEM(BLOCK, jnp.float32),
            pltpu.VMEM(BLOCK, jnp.float32),
            pltpu.VMEM((2,) + BLOCK, jnp.float32),
            pltpu.VMEM((2,) + BLOCK, jnp.float32),
            pltpu.VMEM(BLOCK, jnp.float32),
        ],
        compiler_params=PARAMS,
        name="steps",
    )(spacing_index, strength_index, obs_offsets, own, nat, d, near, far)

    edge = lax.ppermute(edge, "tile", [(i, (i + 1) % TILES) for i in range(TILES)])
    sums = lax.all_to_all(sums, "tile", 0, 0)

    out, misfit = pl.pallas_call(
        last_kernel,
        out_shape=(f32(*BLOCK), f32(1)),
        in_specs=[SM] + [VM] * 5,
        out_specs=(VM, SM),
        scratch_shapes=[pltpu.VMEM(BLOCK, jnp.float32)],
        compiler_params=PARAMS,
        name="last",
    )(strength_index, own2, beyond, edge, d2, sums)
    return out[None], misfit


def solution(mesh):
    placed = (P("run", None, None, "tile", None), P("run"), P("run"), P())
    return jax.shard_map(
        shards,
        mesh=mesh,
        in_specs=placed,
        out_specs=(P("run", None, None, "tile", None), P("run")),
        check_vma=False,
    )
```

```python
import jax
import jax.numpy as jnp
from jax import lax
from jax.experimental import pallas as pl
from jax.experimental.pallas import tpu as pltpu
from jax.sharding import PartitionSpec as P

RUNS = 16
TILES = 32
PLANES = 8
CELLS = 8 * 256 * 128

DT = 0.05
VISC = 0.05
GAMMA1 = 0.4
GRAVITY = 0.5
HOT = 1.2
COLD = 0.8

ROWS = (8, 128)
UNROLL = 2


def rolled(v, shift, axis):
    return pltpu.roll(v, shift % v.shape[axis], axis)


def sub_ids():
    return lax.broadcasted_iota(jnp.int32, ROWS, 0)


def lane_ids():
    return lax.broadcasted_iota(jnp.int32, ROWS, 1)


class Spread:
    def __init__(self, sp_ref, off_ref):
        sub, lane = sub_ids(), lane_ids()
        k = sp_ref[0]
        self.off = off_ref
        self.sub_odd = (sub & 1) == 1
        self.lane_odd = (lane & 1) == 1
        self.masks = []
        for ids in (sub, lane):
            self.masks.append(
                tuple(((ids & bit) != 0) & (k >= level) for bit, level in ((2, 2), (4, 3)))
            )
        self.sub1, self.lane1 = sub & 1, lane & 1

    def plane(self, z):
        return self.sub1 == self.off[z, 0], self.lane1 == self.off[z, 1]

    def __call__(self, e, keep):
        for axis in (0, 1):
            odd = (self.sub_odd, self.lane_odd)[axis]
            swapped = jnp.where(odd, rolled(e, 1, axis), rolled(e, -1, axis))
            e = jnp.where(keep[axis], e, swapped)
            for mask, shift in zip(self.masks[axis], (2, 4)):
                e = jnp.where(mask, rolled(e, shift, axis), e)
        return e


def ghosted(load):
    def get(c, z, t):
        if z < 0:
            edge = load(c, 0, t)
            return edge if c < 3 else -edge if c == 3 else 2.0 * HOT - edge
        if z >= PLANES:
            edge = load(c, PLANES - 1, t)
            return edge if c < 3 else -edge if c == 3 else 2.0 * COLD - edge
        return load(c, z, t)

    return get


def neighbours_x(a, b, sub):
    a1, b1 = rolled(a, -1, 0), rolled(b, -1, 0)
    a2, b2 = rolled(a, 1, 0), rolled(b, 1, 0)
    last, first = sub == 7, sub == 0
    return (
        (jnp.where(last, b1, a1), jnp.where(last, a1, b1)),
        (jnp.where(first, b2, a2), jnp.where(first, a2, b2)),
    )


def stepped(get, z, tiles, sub):
    centre = [[get(c, z, t) for t in (0, 1)] for c in range(5)]
    along_x = [neighbours_x(v[0], v[1], sub) for v in centre]
    result = []
    for t in tiles:
        c0 = [v[t] for v in centre]
        xn = [v[0][t] for v in along_x]
        xp = [v[1][t] for v in along_x]
        yn = [rolled(v, -1, 1) for v in c0]
        yp = [rolled(v, 1, 1) for v in c0]
        zn = [get(c, z + 1, t) for c in range(5)]
        zp = [get(c, z - 1, t) for c in range(5)]
        flux = (
            (xn[0] * xn[1] - xp[0] * xp[1])
            + (yn[0] * yn[2] - yp[0] * yp[2])
            + (zn[0] * zn[3] - zp[0] * zp[3])
        )
        scale = (0.5 * DT) / c0[0]
        grad = (
            xn[0] * xn[4] - xp[0] * xp[4],
            yn[0] * yn[4] - yp[0] * yp[4],
            zn[0] * zn[4] - zp[0] * zp[4],
        )
        new = [c0[0] - (0.5 * DT) * flux]
        div = None
        for q in range(1, 5):
            dx, dy, dz = xn[q] - xp[q], yn[q] - yp[q], zn[q] - zp[q]
            part = (None, dx, dy, dz, None)[q]
            if part is not None:
                div = part if div is None else div + part
            adv = c0[1] * dx + c0[2] * dy + c0[3] * dz
            six = ((xn[q] + xp[q]) + (yn[q] + yp[q])) + (zn[q] + zp[q])
            change = (DT * VISC) * (six - 6.0 * c0[q]) - (0.5 * DT) * adv
            if q < 4:
                change = change - grad[q - 1] * scale
                if q == 3:
                    change = change - DT * GRAVITY
            else:
                change = change - (0.5 * DT * GAMMA1) * (c0[4] * div)
            new.append(c0[q] + change)
        result.append(new)
    return result


def nudge_factor(st_ref):
    strength = 0.5 * lax.shift_left(jnp.int32(1), st_ref[0]).astype(jnp.float32)
    return jnp.where(lax.axis_index("run") == 0, 0.0, DT * strength)


def pack_kernel(sp_ref, off_ref, own_ref, y_ref, p_ref, q_ref, nat_ref, d_ref, near_ref, far_ref):
    spread = Spread(sp_ref, off_ref)
    sub = sub_ids()
    even = lax.rem(lax.axis_index("tile"), 2) == 0
    to_near = (sub >= 4) == even
    for z in range(PLANES):
        keep = spread.plane(z)
        for c in range(5):
            own = own_ref[c, z]
            nat = y_ref[c, z] + p_ref[c, z] + q_ref[c, z]
            nat_ref[c, z] = nat
            if c > 0:
                d = spread(own - nat, keep)
                d_ref[c - 1, z] = d
                own = jnp.where(sub == 5, rolled(d, -2, 0), own)
            other = rolled(nat, 4, 0)
            near_ref[c, z] = jnp.where(to_near, own, other)
            far_ref[c, z] = jnp.where(to_near, other, own)


def set_ghosts(ref):
    for c in range(5):
        for t in (0, 1):
            low, high = ref[c, 1, t], ref[c, PLANES, t]
            if c == 3:
                low, high = -low, -high
            elif c == 4:
                low, high = 2.0 * HOT - low, 2.0 * COLD - high
            ref[c, 0, t] = low
            ref[c, PLANES + 1, t] = high


def steps_kernel(
    sp_ref, st_ref, off_ref, own_ref, nat_ref, d_ref, near_ref, far_ref,
    own2_ref, beyond_ref, edge_ref, d2_ref, sum_ref, a_ref, b_ref, a1_ref, b1_ref, far2_ref, total_ref,
):
    spread = Spread(sp_ref, off_ref)
    sub = sub_ids()
    even = lax.rem(lax.axis_index("tile"), 2) == 0
    from_near = (sub < 4) == even
    mu = nudge_factor(st_ref)
    for z in range(PLANES):
        for c in range(5):
            near, far = near_ref[c, z], far_ref[c, z]
            a_ref[c, z + 1, 0] = own_ref[c, z]
            b_ref[c, z + 1, 0] = nat_ref[c, z]
            a_ref[c, z + 1, 1] = jnp.where(from_near, near, far)
            b_ref[c, z + 1, 1] = rolled(jnp.where(from_near, far, near), 4, 0)
    set_ghosts(a_ref)
    set_ghosts(b_ref)

    def getter(ref):
        return lambda c, z, t: ref[c, z + 1, t]

    def first(z):
        keep = spread.plane(z)
        new_a = stepped(getter(a_ref), z, (0, 1), sub)
        new_b = stepped(getter(b_ref), z, (0, 1), sub)
        for t in (0, 1):
            for c in range(5):
                value = new_a[t][c]
                if c > 0:
                    if t == 0:
                        d = d_ref[c - 1, z]
                    else:
                        halo = a_ref[c, z + 1, 1]
                        d = spread(halo - b_ref[c, z + 1, 1], keep)
                        d = jnp.where(sub == 7, rolled(halo, 2, 0), d)
                    value = value - mu * d
                a1_ref[c, z + 1, t] = value
                b1_ref[c, z + 1, t] = new_b[t][c]

    def second(z):
        keep = spread.plane(z)
        new_a = stepped(getter(a1_ref), z, (0, 1), sub)
        new_b = stepped(getter(b1_ref), z, (0,), sub)[0]
        for c in range(5):
            for t in (0, 1):
                value = new_a[t][c]
                if c > 0:
                    value = value - mu * spread(a1_ref[c, z + 1, t] - b1_ref[c, z + 1, t], keep)
                if t == 0:
                    own2_ref[c, z] = value
                    if c > 0:
                        d = spread(value - new_b[c], keep)
                        d2_ref[c - 1, z] = d
                        if c == 4:
                            total_ref[...] += d * d
                else:
                    far2_ref[c, z] = value

    def planes(body):
        def several(i, carry):
            for k in range(UNROLL):
                body(i * UNROLL + k)
            return carry

        lax.fori_loop(0, PLANES // UNROLL, several, 0)

    total_ref[...] = jnp.zeros(ROWS, jnp.float32)
    planes(first)
    set_ghosts(a1_ref)
    set_ghosts(b1_ref)
    planes(second)
    for c in range(5):
        for z in range(PLANES):
            edge_ref[c, z : z + 1] = own2_ref[c, z, 7:8]
            beyond_ref[c, z : z + 1] = far2_ref[c, z, 0:1]
    total = jnp.sum(total_ref[...], axis=0)
    sum_ref[...] = jnp.broadcast_to(total[None, None], sum_ref.shape)


def last_kernel(st_ref, own_ref, beyond_ref, edge_ref, d_ref, sums_ref, out_ref, misfit_ref, h_ref):
    sub = sub_ids()
    mu = nudge_factor(st_ref)
    for c in range(5):
        for z in range(PLANES):
            h_ref[c, z] = jnp.where(
                sub == 0,
                jnp.broadcast_to(beyond_ref[c, z : z + 1], ROWS),
                jnp.broadcast_to(edge_ref[c, z : z + 1], ROWS),
            )
    a = ghosted(lambda c, z, t: h_ref[c, z] if t else own_ref[c, z])
    for z in range(PLANES):
        new = stepped(a, z, (0,), sub)[0]
        for c in range(5):
            value = new[c]
            if c > 0:
                value = value - mu * d_ref[c - 1, z]
            out_ref[c, z] = value
    misfit_ref[0] = jnp.sum(sums_ref[...]) * (1.0 / CELLS)


def f32(*shape):
    return jax.ShapeDtypeStruct(shape, jnp.float32)


VM = pl.BlockSpec(memory_space=pltpu.VMEM)
SM = pl.BlockSpec(memory_space=pltpu.SMEM)
PARAMS = pltpu.CompilerParams(vmem_limit_bytes=12 * 2**20)
BLOCK = (5, PLANES, 8, 128)
BLOCK4 = (4, PLANES, 8, 128)
EXTENDED = (5, PLANES + 2, 2, 8, 128)


def twice(pairs):
    return pairs + [(a + 8, b + 8) for a, b in pairs]


def shards(state, spacing_index, strength_index, obs_offsets):
    own = state[0]
    run = lax.axis_index("run")

    p = lax.ppermute(own, "run", [(0, 8)])
    y = jnp.where(run == 0, own, p)
    p = lax.ppermute(y, "run", twice([(0, 3)]))
    q = lax.ppermute(y, "run", twice([(0, 5)]))
    y = y + p + q
    p = lax.ppermute(y, "run", twice([(0, 1), (3, 4), (5, 6)]))
    q = lax.ppermute(y, "run", twice([(0, 7), (3, 2)]))

    nat, d, near, far = pl.pallas_call(
        pack_kernel,
        out_shape=(f32(*BLOCK), f32(*BLOCK4), f32(*BLOCK), f32(*BLOCK)),
        in_specs=[SM, SM, VM, VM, VM, VM],
        out_specs=(VM,) * 4,
        compiler_params=PARAMS,
        name="pack",
    )(spacing_index, obs_offsets, own, y, p, q)

    far = lax.ppermute(
        far, "tile", [(i, (i + 1) % TILES if i % 2 else (i - 1) % TILES) for i in range(TILES)]
    )
    near = lax.ppermute(near, "tile", [(i, i ^ 1) for i in range(TILES)])

    own2, beyond, edge, d2, sums = pl.pallas_call(
        steps_kernel,
        out_shape=(
            f32(*BLOCK), f32(5, PLANES, 128), f32(5, PLANES, 128), f32(*BLOCK4), f32(TILES, 1, 128)
        ),
        in_specs=[SM, SM, SM] + [VM] * 5,
        out_specs=(VM,) * 5,
        scratch_shapes=[
            *[pltpu.VMEM(EXTENDED, jnp.float32)] * 4,
            pltpu.VMEM(BLOCK, jnp.float32),
            pltpu.VMEM(ROWS, jnp.float32),
        ],
        compiler_params=PARAMS,
        name="steps",
    )(spacing_index, strength_index, obs_offsets, own, nat, d, near, far)

    edge = lax.ppermute(edge, "tile", [(i, (i + 1) % TILES) for i in range(TILES)])
    sums = lax.all_to_all(sums, "tile", 0, 0)

    out, misfit = pl.pallas_call(
        last_kernel,
        out_shape=(f32(*BLOCK), f32(1)),
        in_specs=[SM] + [VM] * 5,
        out_specs=(VM, SM),
        scratch_shapes=[pltpu.VMEM(BLOCK, jnp.float32)],
        compiler_params=PARAMS,
        name="last",
    )(strength_index, own2, beyond, edge, d2, sums)
    return out[None], misfit


def solution(mesh):
    placed = (P("run", None, None, "tile", None), P("run"), P("run"), P())
    return jax.shard_map(
        shards,
        mesh=mesh,
        in_specs=placed,
        out_specs=(P("run", None, None, "tile", None), P("run")),
        check_vma=False,
    )
```

```python
import jax
import jax.numpy as jnp
from jax import lax
from jax.experimental import pallas as pl
from jax.experimental.pallas import tpu as pltpu
from jax.sharding import PartitionSpec as P

RUNS = 16
TILES = 32
PLANES = 8
CELLS = 8 * 256 * 128

DT = 0.05
VISC = 0.05
GAMMA1 = 0.4
GRAVITY = 0.5
HOT = 1.2
COLD = 0.8

ROWS = (8, 128)
UNROLL = 2


def rolled(v, shift, axis):
    return pltpu.roll(v, shift % v.shape[axis], axis)


def sub_ids():
    return lax.broadcasted_iota(jnp.int32, ROWS, 0)


def lane_ids():
    return lax.broadcasted_iota(jnp.int32, ROWS, 1)


class Spread:
    def __init__(self, sp_ref, off_ref):
        k = sp_ref[0]
        self.off = off_ref
        self.base = [lax.shift_left(lax.shift_right_logical(ids, k), k) for ids in (sub_ids(), lane_ids())]

    def plane(self, z):
        return self.base[0] + self.off[z, 0], self.base[1] + self.off[z, 1]

    def __call__(self, e, index):
        for axis in (0, 1):
            e = jnp.take_along_axis(e, index[axis], axis=axis, mode="promise_in_bounds")
        return e


def put(ref, c, z, t, value):
    ref[c, z + 1, 8 + 8 * t : 16 + 8 * t] = value
    if t == 0:
        ref[c, z + 1, 24:25] = value[0:1]
    else:
        ref[c, z + 1, 7:8] = value[7:8]


def get(ref, c, z, t, shift=0):
    first = 8 + 8 * t + shift
    return ref[c, z + 1, first : first + 8]


def set_ghosts(ref, tiles=(0, 1)):
    for c in range(5):
        for t in tiles:
            low, high = get(ref, c, 0, t), get(ref, c, PLANES - 1, t)
            if c == 3:
                low, high = -low, -high
            elif c == 4:
                low, high = 2.0 * HOT - low, 2.0 * COLD - high
            ref[c, 0, 8 + 8 * t : 16 + 8 * t] = low
            ref[c, PLANES + 1, 8 + 8 * t : 16 + 8 * t] = high


def stepped(ref, z, t):
    c0, xn, xp, zn, zp = (
        [get(ref, c, z + dz, t, dx) for c in range(5)]
        for dz, dx in ((0, 0), (0, 1), (0, -1), (1, 0), (-1, 0))
    )
    yn = [rolled(v, -1, 1) for v in c0]
    yp = [rolled(v, 1, 1) for v in c0]
    flux = (
        (xn[0] * xn[1] - xp[0] * xp[1])
        + (yn[0] * yn[2] - yp[0] * yp[2])
        + (zn[0] * zn[3] - zp[0] * zp[3])
    )
    scale = (0.5 * DT) / c0[0]
    grad = (
        xn[0] * xn[4] - xp[0] * xp[4],
        yn[0] * yn[4] - yp[0] * yp[4],
        zn[0] * zn[4] - zp[0] * zp[4],
    )
    new = [c0[0] - (0.5 * DT) * flux]
    div = None
    for q in range(1, 5):
        dx, dy, dz = xn[q] - xp[q], yn[q] - yp[q], zn[q] - zp[q]
        part = (None, dx, dy, dz, None)[q]
        if part is not None:
            div = part if div is None else div + part
        adv = c0[1] * dx + c0[2] * dy + c0[3] * dz
        six = ((xn[q] + xp[q]) + (yn[q] + yp[q])) + (zn[q] + zp[q])
        change = (DT * VISC) * (six - 6.0 * c0[q]) - (0.5 * DT) * adv
        if q < 4:
            change = change - grad[q - 1] * scale
            if q == 3:
                change = change - DT * GRAVITY
        else:
            change = change - (0.5 * DT * GAMMA1) * (c0[4] * div)
        new.append(c0[q] + change)
    return new


def nudge_factor(st_ref):
    strength = 0.5 * lax.shift_left(jnp.int32(1), st_ref[0]).astype(jnp.float32)
    return jnp.where(lax.axis_index("run") == 0, 0.0, DT * strength)


def pack_kernel(sp_ref, off_ref, own_ref, y_ref, p_ref, q_ref, nat_ref, d_ref, near_ref, far_ref):
    spread = Spread(sp_ref, off_ref)
    sub = sub_ids()
    even = lax.rem(lax.axis_index("tile"), 2) == 0
    to_near = (sub >= 4) == even
    for z in range(PLANES):
        keep = spread.plane(z)
        for c in range(5):
            own = own_ref[c, z]
            nat = y_ref[c, z] + p_ref[c, z] + q_ref[c, z]
            nat_ref[c, z] = nat
            if c > 0:
                d = spread(own - nat, keep)
                d_ref[c - 1, z] = d
                own = jnp.where(sub == 5, rolled(d, -2, 0), own)
            other = rolled(nat, 4, 0)
            near_ref[c, z] = jnp.where(to_near, own, other)
            far_ref[c, z] = jnp.where(to_near, other, own)


def steps_kernel(
    sp_ref, st_ref, off_ref, own_ref, nat_ref, d_ref, far_ref, near_ref,
    own2_ref, beyond_ref, edge_ref, d2_ref, sum_ref, a_ref, b_ref, a1_ref, b1_ref, far2_ref, total_ref,
):
    spread = Spread(sp_ref, off_ref)
    sub = sub_ids()
    even = lax.rem(lax.axis_index("tile"), 2) == 0
    from_near = (sub < 4) == even
    mu = nudge_factor(st_ref)
    for z in range(PLANES):
        for c in range(5):
            near, far = near_ref[c, z], far_ref[c, z]
            put(a_ref, c, z, 0, own_ref[c, z])
            put(b_ref, c, z, 0, nat_ref[c, z])
            put(a_ref, c, z, 1, jnp.where(from_near, near, far))
            put(b_ref, c, z, 1, rolled(jnp.where(from_near, far, near), 4, 0))
    set_ghosts(a_ref)
    set_ghosts(b_ref)

    def first(z):
        index = spread.plane(z)
        for t in (0, 1):
            new_a = stepped(a_ref, z, t)
            new_b = stepped(b_ref, z, t)
            for c in range(5):
                value = new_a[c]
                if c > 0:
                    if t == 0:
                        d = d_ref[c - 1, z]
                    else:
                        halo = get(a_ref, c, z, 1)
                        d = spread(halo - get(b_ref, c, z, 1), index)
                        d = jnp.where(sub == 7, rolled(halo, 2, 0), d)
                    value = value - mu * d
                put(a1_ref, c, z, t, value)
                put(b1_ref, c, z, t, new_b[c])

    def second(z):
        index = spread.plane(z)
        new_b = stepped(b1_ref, z, 0)
        for t in (0, 1):
            new_a = stepped(a1_ref, z, t)
            for c in range(5):
                value = new_a[c]
                if c > 0:
                    value = value - mu * spread(get(a1_ref, c, z, t) - get(b1_ref, c, z, t), index)
                if t == 0:
                    own2_ref[c, z] = value
                    if c > 0:
                        d = spread(value - new_b[c], index)
                        d2_ref[c - 1, z] = d
                        if c == 4:
                            total_ref[...] += d * d
                else:
                    far2_ref[c, z] = value

    def planes(body):
        def several(i, carry):
            for k in range(UNROLL):
                body(i * UNROLL + k)
            return carry

        lax.fori_loop(0, PLANES // UNROLL, several, 0)

    total_ref[...] = jnp.zeros(ROWS, jnp.float32)
    planes(first)
    set_ghosts(a1_ref)
    set_ghosts(b1_ref, (0,))
    planes(second)
    for c in range(5):
        for z in range(PLANES):
            edge_ref[c, z : z + 1] = own2_ref[c, z, 7:8]
            beyond_ref[c, z : z + 1] = far2_ref[c, z, 0:1]
    total = jnp.sum(total_ref[...], axis=0)
    sum_ref[...] = jnp.broadcast_to(total[None, None], sum_ref.shape)


def last_kernel(st_ref, own_ref, beyond_ref, edge_ref, d_ref, sums_ref, out_ref, misfit_ref, a_ref):
    mu = nudge_factor(st_ref)
    for c in range(5):
        for z in range(PLANES):
            a_ref[c, z + 1, 8:16] = own_ref[c, z]
            a_ref[c, z + 1, 7:8] = edge_ref[c, z : z + 1]
            a_ref[c, z + 1, 16:17] = beyond_ref[c, z : z + 1]
    set_ghosts(a_ref, (0,))
    for z in range(PLANES):
        new = stepped(a_ref, z, 0)
        for c in range(5):
            value = new[c]
            if c > 0:
                value = value - mu * d_ref[c - 1, z]
            out_ref[c, z] = value
    misfit_ref[0] = jnp.sum(sums_ref[...]) * (1.0 / CELLS)


def f32(*shape):
    return jax.ShapeDtypeStruct(shape, jnp.float32)


VM = pl.BlockSpec(memory_space=pltpu.VMEM)
SM = pl.BlockSpec(memory_space=pltpu.SMEM)
PARAMS = pltpu.CompilerParams(vmem_limit_bytes=12 * 2**20)
BLOCK = (5, PLANES, 8, 128)
BLOCK4 = (4, PLANES, 8, 128)
EXTENDED = (5, PLANES + 2, 32, 128)


def twice(pairs):
    return pairs + [(a + 8, b + 8) for a, b in pairs]


def shards(state, spacing_index, strength_index, obs_offsets):
    own = state[0]
    run = lax.axis_index("run")

    p = lax.ppermute(own, "run", [(0, 8)])
    y = jnp.where(run == 0, own, p)
    p = lax.ppermute(y, "run", twice([(0, 3)]))
    q = lax.ppermute(y, "run", twice([(0, 5)]))
    y = y + p + q
    p = lax.ppermute(y, "run", twice([(0, 1), (3, 4), (5, 6)]))
    q = lax.ppermute(y, "run", twice([(0, 7), (3, 2)]))

    nat, d, near, far = pl.pallas_call(
        pack_kernel,
        out_shape=(f32(*BLOCK), f32(*BLOCK4), f32(*BLOCK), f32(*BLOCK)),
        in_specs=[SM, SM, VM, VM, VM, VM],
        out_specs=(VM,) * 4,
        compiler_params=PARAMS,
        name="pack",
    )(spacing_index, obs_offsets, own, y, p, q)

    far = lax.ppermute(
        far, "tile", [(i, (i + 1) % TILES if i % 2 else (i - 1) % TILES) for i in range(TILES)]
    )
    near = lax.ppermute(near, "tile", [(i, i ^ 1) for i in range(TILES)])

    own2, beyond, edge, d2, sums = pl.pallas_call(
        steps_kernel,
        out_shape=(
            f32(*BLOCK), f32(5, PLANES, 128), f32(5, PLANES, 128), f32(*BLOCK4), f32(TILES, 1, 128)
        ),
        in_specs=[SM, SM, SM] + [VM] * 5,
        out_specs=(VM,) * 5,
        scratch_shapes=[
            *[pltpu.VMEM(EXTENDED, jnp.float32)] * 4,
            pltpu.VMEM(BLOCK, jnp.float32),
            pltpu.VMEM(ROWS, jnp.float32),
        ],
        compiler_params=PARAMS,
        name="steps",
    )(spacing_index, strength_index, obs_offsets, own, nat, d, far, near)

    edge = lax.ppermute(edge, "tile", [(i, (i + 1) % TILES) for i in range(TILES)])
    sums = lax.all_to_all(sums, "tile", 0, 0)

    out, misfit = pl.pallas_call(
        last_kernel,
        out_shape=(f32(*BLOCK), f32(1)),
        in_specs=[SM] + [VM] * 5,
        out_specs=(VM, SM),
        scratch_shapes=[pltpu.VMEM(EXTENDED, jnp.float32)],
        compiler_params=PARAMS,
        name="last",
    )(strength_index, own2, beyond, edge, d2, sums)
    return out[None], misfit


def solution(mesh):
    placed = (P("run", None, None, "tile", None), P("run"), P("run"), P())
    return jax.shard_map(
        shards,
        mesh=mesh,
        in_specs=placed,
        out_specs=(P("run", None, None, "tile", None), P("run")),
        check_vma=False,
    )
```

```python
import jax
import jax.numpy as jnp
from jax import lax
from jax.experimental import pallas as pl
from jax.experimental.pallas import tpu as pltpu
from jax.sharding import PartitionSpec as P

RUNS = 16
TILES = 32
PLANES = 8
CELLS = 8 * 256 * 128

DT = 0.05
VISC = 0.05
GAMMA1 = 0.4
GRAVITY = 0.5
HOT = 1.2
COLD = 0.8

ROWS = (8, 128)
UNROLL = 2


def rolled(v, shift, axis):
    return pltpu.roll(v, shift % v.shape[axis], axis)


def sub_ids():
    return lax.broadcasted_iota(jnp.int32, ROWS, 0)


def lane_ids():
    return lax.broadcasted_iota(jnp.int32, ROWS, 1)


class Spread:
    def __init__(self, sp_ref, off_ref):
        k = sp_ref[0]
        self.off = off_ref
        self.base = [lax.shift_left(lax.shift_right_logical(ids, k), k) for ids in (sub_ids(), lane_ids())]

    def plane(self, z):
        return self.base[0] + self.off[z, 0], self.base[1] + self.off[z, 1]

    def __call__(self, e, index):
        for axis in (0, 1):
            e = jnp.take_along_axis(e, index[axis], axis=axis, mode="promise_in_bounds")
        return e


def put(ref, c, z, t, value):
    ref[c, z + 1, 8 + 8 * t : 16 + 8 * t] = value
    if t == 0:
        ref[c, z + 1, 24:25] = value[0:1]
    else:
        ref[c, z + 1, 7:8] = value[7:8]


def get(ref, c, z, t, shift=0):
    first = 8 + 8 * t + shift
    return ref[c, z + 1, first : first + 8]


def set_ghosts(ref, tiles=(0, 1)):
    for c in range(5):
        for t in tiles:
            low, high = get(ref, c, 0, t), get(ref, c, PLANES - 1, t)
            if c == 3:
                low, high = -low, -high
            elif c == 4:
                low, high = 2.0 * HOT - low, 2.0 * COLD - high
            ref[c, 0, 8 + 8 * t : 16 + 8 * t] = low
            ref[c, PLANES + 1, 8 + 8 * t : 16 + 8 * t] = high


def stepped(ref, z, t):
    c0, xn, xp, zn, zp = (
        [get(ref, c, z + dz, t, dx) for c in range(5)]
        for dz, dx in ((0, 0), (0, 1), (0, -1), (1, 0), (-1, 0))
    )
    yn = [rolled(v, -1, 1) for v in c0]
    yp = [rolled(v, 1, 1) for v in c0]
    flux = (
        (xn[0] * xn[1] - xp[0] * xp[1])
        + (yn[0] * yn[2] - yp[0] * yp[2])
        + (zn[0] * zn[3] - zp[0] * zp[3])
    )
    scale = (0.5 * DT) / c0[0]
    grad = (
        xn[0] * xn[4] - xp[0] * xp[4],
        yn[0] * yn[4] - yp[0] * yp[4],
        zn[0] * zn[4] - zp[0] * zp[4],
    )
    new = [c0[0] - (0.5 * DT) * flux]
    div = None
    for q in range(1, 5):
        dx, dy, dz = xn[q] - xp[q], yn[q] - yp[q], zn[q] - zp[q]
        part = (None, dx, dy, dz, None)[q]
        if part is not None:
            div = part if div is None else div + part
        adv = c0[1] * dx + c0[2] * dy + c0[3] * dz
        six = ((xn[q] + xp[q]) + (yn[q] + yp[q])) + (zn[q] + zp[q])
        change = (DT * VISC) * (six - 6.0 * c0[q]) - (0.5 * DT) * adv
        if q < 4:
            change = change - grad[q - 1] * scale
            if q == 3:
                change = change - DT * GRAVITY
        else:
            change = change - (0.5 * DT * GAMMA1) * (c0[4] * div)
        new.append(c0[q] + change)
    return new


def nudge_factor(st_ref):
    strength = 0.5 * lax.shift_left(jnp.int32(1), st_ref[0]).astype(jnp.float32)
    return jnp.where(lax.axis_index("run") == 0, 0.0, DT * strength)


def pack_kernel(sp_ref, off_ref, own_ref, y_ref, u_ref, v_ref, p_ref, e_ref, h_ref, nat_ref, d_ref, near_ref, far_ref):
    spread = Spread(sp_ref, off_ref)
    sub = sub_ids()
    even = lax.rem(lax.axis_index("tile"), 2) == 0
    to_near = (sub >= 4) == even
    root = lax.axis_index("run") == 0
    for z in range(PLANES):
        keep = spread.plane(z)
        for c in range(5):
            own = own_ref[c, z]
            nat = (y_ref[c, z] + u_ref[c, z] + v_ref[c, z]) + (p_ref[c, z] + e_ref[c, z] + h_ref[c, z])
            nat = jnp.where(root, own, nat)
            nat_ref[c, z] = nat
            if c > 0:
                d = spread(own - nat, keep)
                d_ref[c - 1, z] = d
                own = jnp.where(sub == 5, rolled(d, -2, 0), own)
            other = rolled(nat, 4, 0)
            near_ref[c, z] = jnp.where(to_near, own, other)
            far_ref[c, z] = jnp.where(to_near, other, own)


def steps_kernel(
    sp_ref, st_ref, off_ref, own_ref, nat_ref, d_ref, near_ref, far_ref,
    own2_ref, beyond_ref, edge_ref, d2_ref, sum_ref, a_ref, b_ref, a1_ref, b1_ref, far2_ref, total_ref,
):
    spread = Spread(sp_ref, off_ref)
    sub = sub_ids()
    even = lax.rem(lax.axis_index("tile"), 2) == 0
    from_near = (sub < 4) == even
    mu = nudge_factor(st_ref)
    for z in range(PLANES):
        for c in range(5):
            near, far = near_ref[c, z], far_ref[c, z]
            put(a_ref, c, z, 0, own_ref[c, z])
            put(b_ref, c, z, 0, nat_ref[c, z])
            put(a_ref, c, z, 1, jnp.where(from_near, near, far))
            put(b_ref, c, z, 1, rolled(jnp.where(from_near, far, near), 4, 0))
    set_ghosts(a_ref)
    set_ghosts(b_ref)

    def first(z):
        index = spread.plane(z)
        for t in (0, 1):
            new_a = stepped(a_ref, z, t)
            new_b = stepped(b_ref, z, t)
            for c in range(5):
                value = new_a[c]
                if c > 0:
                    if t == 0:
                        d = d_ref[c - 1, z]
                    else:
                        halo = get(a_ref, c, z, 1)
                        d = spread(halo - get(b_ref, c, z, 1), index)
                        d = jnp.where(sub == 7, rolled(halo, 2, 0), d)
                    value = value - mu * d
                put(a1_ref, c, z, t, value)
                put(b1_ref, c, z, t, new_b[c])

    def second(z):
        index = spread.plane(z)
        new_b = stepped(b1_ref, z, 0)
        for t in (0, 1):
            new_a = stepped(a1_ref, z, t)
            for c in range(5):
                value = new_a[c]
                if c > 0:
                    value = value - mu * spread(get(a1_ref, c, z, t) - get(b1_ref, c, z, t), index)
                if t == 0:
                    own2_ref[c, z] = value
                    if c > 0:
                        d = spread(value - new_b[c], index)
                        d2_ref[c - 1, z] = d
                        if c == 4:
                            total_ref[...] += d * d
                else:
                    far2_ref[c, z] = value

    def planes(body):
        def several(i, carry):
            for k in range(UNROLL):
                body(i * UNROLL + k)
            return carry

        lax.fori_loop(0, PLANES // UNROLL, several, 0)

    total_ref[...] = jnp.zeros(ROWS, jnp.float32)
    planes(first)
    set_ghosts(a1_ref)
    set_ghosts(b1_ref, (0,))
    planes(second)
    for c in range(5):
        for z in range(PLANES):
            edge_ref[c, z : z + 1] = own2_ref[c, z, 7:8]
            beyond_ref[c, z : z + 1] = far2_ref[c, z, 0:1]
    total = jnp.sum(total_ref[...], axis=0)
    sum_ref[...] = jnp.broadcast_to(total[None, None], sum_ref.shape)


def last_kernel(st_ref, own_ref, beyond_ref, edge_ref, d_ref, sums_ref, out_ref, misfit_ref, a_ref):
    mu = nudge_factor(st_ref)
    for c in range(5):
        for z in range(PLANES):
            a_ref[c, z + 1, 8:16] = own_ref[c, z]
            a_ref[c, z + 1, 7:8] = edge_ref[c, z : z + 1]
            a_ref[c, z + 1, 16:17] = beyond_ref[c, z : z + 1]
    set_ghosts(a_ref, (0,))
    for z in range(PLANES):
        new = stepped(a_ref, z, 0)
        for c in range(5):
            value = new[c]
            if c > 0:
                value = value - mu * d_ref[c - 1, z]
            out_ref[c, z] = value
    misfit_ref[0] = jnp.sum(sums_ref[...]) * (1.0 / CELLS)


def f32(*shape):
    return jax.ShapeDtypeStruct(shape, jnp.float32)


VM = pl.BlockSpec(memory_space=pltpu.VMEM)
SM = pl.BlockSpec(memory_space=pltpu.SMEM)
PARAMS = pltpu.CompilerParams(vmem_limit_bytes=12 * 2**20)
BLOCK = (5, PLANES, 8, 128)
BLOCK4 = (4, PLANES, 8, 128)
EXTENDED = (5, PLANES + 2, 32, 128)


def shards(state, spacing_index, strength_index, obs_offsets):
    own = state[0]

    def send(x, pairs):
        return lax.ppermute(x, "run", pairs)

    p = send(own, [(0, 8)])
    a, b, e = send(own, [(0, 2)]), send(own, [(0, 6)]), send(own, [(0, 4)])
    f, g, h = send(p, [(8, 10)]), send(p, [(8, 14)]), send(p, [(8, 12)])
    y = a + b + f + g
    u = send(y, [(2, 3), (6, 7), (10, 11), (14, 15)])
    v = send(y, [(2, 1), (6, 5), (10, 9), (14, 13)])

    nat, d, near, far = pl.pallas_call(
        pack_kernel,
        out_shape=(f32(*BLOCK), f32(*BLOCK4), f32(*BLOCK), f32(*BLOCK)),
        in_specs=[SM, SM] + [VM] * 7,
        out_specs=(VM,) * 4,
        compiler_params=PARAMS,
        name="pack",
    )(spacing_index, obs_offsets, own, y, u, v, p, e, h)

    far = lax.ppermute(
        far, "tile", [(i, (i + 1) % TILES if i % 2 else (i - 1) % TILES) for i in range(TILES)]
    )
    near = lax.ppermute(near, "tile", [(i, i ^ 1) for i in range(TILES)])

    own2, beyond, edge, d2, sums = pl.pallas_call(
        steps_kernel,
        out_shape=(
            f32(*BLOCK), f32(5, PLANES, 128), f32(5, PLANES, 128), f32(*BLOCK4), f32(TILES, 1, 128)
        ),
        in_specs=[SM, SM, SM] + [VM] * 5,
        out_specs=(VM,) * 5,
        scratch_shapes=[
            *[pltpu.VMEM(EXTENDED, jnp.float32)] * 4,
            pltpu.VMEM(BLOCK, jnp.float32),
            pltpu.VMEM(ROWS, jnp.float32),
        ],
        compiler_params=PARAMS,
        name="steps",
    )(spacing_index, strength_index, obs_offsets, own, nat, d, near, far)

    edge = lax.ppermute(edge, "tile", [(i, (i + 1) % TILES) for i in range(TILES)])
    sums = lax.all_to_all(sums, "tile", 0, 0)

    out, misfit = pl.pallas_call(
        last_kernel,
        out_shape=(f32(*BLOCK), f32(1)),
        in_specs=[SM] + [VM] * 5,
        out_specs=(VM, SM),
        scratch_shapes=[pltpu.VMEM(EXTENDED, jnp.float32)],
        compiler_params=PARAMS,
        name="last",
    )(strength_index, own2, beyond, edge, d2, sums)
    return out[None], misfit


def solution(mesh):
    placed = (P("run", None, None, "tile", None), P("run"), P("run"), P())
    return jax.shard_map(
        shards,
        mesh=mesh,
        in_specs=placed,
        out_specs=(P("run", None, None, "tile", None), P("run")),
        check_vma=False,
    )
```

```python
import jax
import jax.numpy as jnp
from jax import lax
from jax.experimental import pallas as pl
from jax.experimental.pallas import tpu as pltpu
from jax.sharding import PartitionSpec as P

RUNS = 16
TILES = 32
PLANES = 8
CELLS = 8 * 256 * 128

DT = 0.05
VISC = 0.05
GAMMA1 = 0.4
GRAVITY = 0.5
HOT = 1.2
COLD = 0.8

ROWS = (8, 128)
UNROLL = 4


def rolled(v, shift, axis):
    return pltpu.roll(v, shift % v.shape[axis], axis)


def sub_ids():
    return lax.broadcasted_iota(jnp.int32, ROWS, 0)


def lane_ids():
    return lax.broadcasted_iota(jnp.int32, ROWS, 1)


class Spread:
    def __init__(self, sp_ref, off_ref):
        k = sp_ref[0]
        self.off = off_ref
        self.base = [lax.shift_left(lax.shift_right_logical(ids, k), k) for ids in (sub_ids(), lane_ids())]

    def plane(self, z):
        return self.base[0] + self.off[z, 0], self.base[1] + self.off[z, 1]

    def __call__(self, e, index):
        for axis in (0, 1):
            e = jnp.take_along_axis(e, index[axis], axis=axis, mode="promise_in_bounds")
        return e


PITCH = 24


def place(z, row):
    return (z + 1) * PITCH + 8 + row


def get(ref, c, z, shift=0):
    return ref[c, pl.ds(place(z, shift), 8)]


def put(ref, c, z, value):
    ref[c, pl.ds(pl.multiple_of(place(z, 0), 8), 8)] = value


def get_edge(ref, c, row):
    return ref[c, pl.ds(place(0, row), PLANES, stride=PITCH)]


def put_edge(ref, c, row, value):
    ref[c, pl.ds(place(0, row), PLANES, stride=PITCH)] = value


def mirrored(c, low, high):
    if c == 3:
        return -low, -high
    if c == 4:
        return 2.0 * HOT - low, 2.0 * COLD - high
    return low, high


def set_ghosts(ref):
    for c in range(5):
        low, high = mirrored(c, get(ref, c, 0), get(ref, c, PLANES - 1))
        put(ref, c, -1, low)
        put(ref, c, PLANES, high)


def advanced(c0, xn, xp, zn, zp):
    yn = [rolled(v, -1, 1) for v in c0]
    yp = [rolled(v, 1, 1) for v in c0]
    flux = (
        (xn[0] * xn[1] - xp[0] * xp[1])
        + (yn[0] * yn[2] - yp[0] * yp[2])
        + (zn[0] * zn[3] - zp[0] * zp[3])
    )
    scale = (0.5 * DT) / c0[0]
    grad = (
        xn[0] * xn[4] - xp[0] * xp[4],
        yn[0] * yn[4] - yp[0] * yp[4],
        zn[0] * zn[4] - zp[0] * zp[4],
    )
    new = [c0[0] - (0.5 * DT) * flux]
    div = None
    for q in range(1, 5):
        dx, dy, dz = xn[q] - xp[q], yn[q] - yp[q], zn[q] - zp[q]
        part = (None, dx, dy, dz, None)[q]
        if part is not None:
            div = part if div is None else div + part
        adv = c0[1] * dx + c0[2] * dy + c0[3] * dz
        six = ((xn[q] + xp[q]) + (yn[q] + yp[q])) + (zn[q] + zp[q])
        change = (DT * VISC) * (six - 6.0 * c0[q]) - (0.5 * DT) * adv
        if q < 4:
            change = change - grad[q - 1] * scale
            if q == 3:
                change = change - DT * GRAVITY
        else:
            change = change - (0.5 * DT * GAMMA1) * (c0[4] * div)
        new.append(c0[q] + change)
    return new


def stepped(ref, z):
    return advanced(
        *([get(ref, c, z + dz, dx) for c in range(5)] for dz, dx in ((0, 0), (0, 1), (0, -1), (1, 0), (-1, 0)))
    )


def edge_stepped(c0, xn, xp):
    sub = sub_ids()
    zn, zp = [], []
    for c in range(5):
        low, high = mirrored(c, c0[c], c0[c])
        zn.append(jnp.where(sub == PLANES - 1, high, rolled(c0[c], -1, 0)))
        zp.append(jnp.where(sub == 0, low, rolled(c0[c], 1, 0)))
    return advanced(c0, xn, xp, zn, zp)


def nudge_factor(st_ref):
    strength = 0.5 * lax.shift_left(jnp.int32(1), st_ref[0]).astype(jnp.float32)
    return jnp.where(lax.axis_index("run") == 0, 0.0, DT * strength)


EDGES = 30


def even_tile():
    return lax.rem(lax.axis_index("tile"), 2) == 0


def tile_of(z):
    return pl.ds(pl.multiple_of(8 * z, 8), 8)


def edge_of(ref, c, row):
    return ref[c, pl.ds(row, PLANES, stride=8)]


def planes(body):
    def several(i, carry):
        for k in range(UNROLL):
            body(i * UNROLL + k)
        return carry

    lax.fori_loop(0, PLANES // UNROLL, several, 0)


def pack_kernel(
    sp_ref, off_ref, own_ref, y_ref, u_ref, v_ref, p_ref, e_ref, h_ref, nat_ref, d_ref, near_ref, far_ref
):
    spread = Spread(sp_ref, off_ref)
    even = even_tile()
    root = lax.axis_index("run") == 0
    for z in range(PLANES):
        index = spread.plane(z)
        here = pl.ds(8 * z, 8)
        for c in range(5):
            own = own_ref[c, here]
            nat = (y_ref[c, here] + u_ref[c, here] + v_ref[c, here]) + (p_ref[c, here] + e_ref[c, here] + h_ref[c, here])
            nat = jnp.where(root, own, nat)
            nat_ref[c, here] = nat
            if c > 0:
                d_ref[c - 1, here] = spread(own - nat, index)
    fields = [(ref, c) for ref in (own_ref, nat_ref) for c in range(5)]
    left = [edge_of(ref, c, row) for ref, c in fields for row in (0, 1, 2)]
    right = [edge_of(ref, c, row) for ref, c in fields for row in (6, 7)] + [edge_of(d_ref, c, 7) for c in range(4)]
    for i in range(EDGES):
        to_right = right[min(i, len(right) - 1)]
        near_ref[i] = jnp.where(even, to_right, left[i])
        far_ref[i] = jnp.where(even, left[i], to_right)


def inner_kernel(st_ref, own_ref, nat_ref, d_ref, own1_ref, nat1_ref, a_ref, b_ref):
    mu = nudge_factor(st_ref)
    for ref, source in ((a_ref, own_ref), (b_ref, nat_ref)):
        for c in range(5):
            for z in range(PLANES):
                put(ref, c, z, source[c, 8 * z : 8 * z + 8])
        set_ghosts(ref)

    def first(z):
        new_a, new_b = stepped(a_ref, z), stepped(b_ref, z)
        for c in range(5):
            own1_ref[c, tile_of(z)] = new_a[c] - mu * d_ref[c - 1, tile_of(z)] if c > 0 else new_a[c]
            nat1_ref[c, tile_of(z)] = new_b[c]

    planes(first)


def steps_kernel(
    sp_ref, st_ref, off_ref, own_ref, nat_ref, d_ref, own1_ref, nat1_ref, near_ref, far_ref,
    own2_ref, beyond_ref, edge_ref, d2_ref, sum_ref, a1_ref, b1_ref, total_ref,
):
    spread = Spread(sp_ref, off_ref)
    even = even_tile()
    mu = nudge_factor(st_ref)
    sub = sub_ids()
    off_x, columns = jnp.zeros(ROWS, jnp.int32), spread.base[1]
    for z in range(PLANES):
        off_x = jnp.where(sub == z, off_ref[z, 0], off_x)
        columns = jnp.where(sub == z, spread.base[1] + off_ref[z, 1], columns)

    def observed(row8, row9):
        return jnp.take_along_axis(
            jnp.where(off_x == 0, row8, row9), columns, axis=1, mode="promise_in_bounds"
        )

    def sent(i, from_left):
        near, far = near_ref[i], far_ref[i]
        return jnp.where(even, far, near) if from_left else jnp.where(even, near, far)

    rows, next_rows = [], []
    for k, ref in ((0, own_ref), (1, nat_ref)):
        row = {
            j: [sent((5 * k + c) * width + i, j < 0) for c in range(5)]
            for j, width, i in ((-2, 2, 0), (-1, 2, 1), (8, 3, 0), (9, 3, 1), (10, 3, 2))
        }
        for j in (0, 1, 6, 7):
            row[j] = [edge_of(ref, c, j) for c in range(5)]
        rows.append(row)
        next_rows.append({j: edge_stepped(row[j], row[j + 1], row[j - 1]) for j in (-1, 0, 7, 8, 9)})
    for c in range(1, 5):
        d = observed(rows[0][8][c] - rows[1][8][c], rows[0][9][c] - rows[1][9][c])
        next_rows[0][-1][c] -= mu * sent(20 + c - 1, True)
        for j in (0, 7):
            next_rows[0][j][c] -= mu * edge_of(d_ref, c - 1, j)
        for j in (8, 9):
            next_rows[0][j][c] -= mu * d
    for ref, source, edge in ((a1_ref, own1_ref, next_rows[0]), (b1_ref, nat1_ref, next_rows[1])):
        for c in range(5):
            for z in range(PLANES):
                put(ref, c, z, source[c, 8 * z : 8 * z + 8])
            for j in (-1, 0, 7, 8):
                put_edge(ref, c, j, edge[j][c])
        set_ghosts(ref)

    def second(z):
        index = spread.plane(z)
        new_a, new_b = stepped(a1_ref, z), stepped(b1_ref, z)
        for c in range(5):
            value = new_a[c]
            if c > 0:
                value = value - mu * spread(get(a1_ref, c, z) - get(b1_ref, c, z), index)
                d = spread(value - new_b[c], index)
                d2_ref[c - 1, z] = d
                if c == 4:
                    total_ref[...] += d * d
            own2_ref[c, tile_of(z)] = value

    total_ref[...] = jnp.zeros(ROWS, jnp.float32)
    planes(second)
    own, nat = next_rows
    new = edge_stepped(own[8], own[9], own[7])
    for c in range(5):
        if c > 0:
            new[c] -= mu * observed(own[8][c] - nat[8][c], own[9][c] - nat[9][c])
        beyond_ref[c] = new[c]
        edge_ref[c] = edge_of(own2_ref, c, 7)
    total = jnp.sum(total_ref[...], axis=0)
    sum_ref[...] = jnp.broadcast_to(total[None, None], sum_ref.shape)


def last_kernel(st_ref, own_ref, beyond_ref, edge_ref, d_ref, sums_ref, out_ref, misfit_ref, a_ref):
    mu = nudge_factor(st_ref)
    for c in range(5):
        for z in range(PLANES):
            put(a_ref, c, z, own_ref[c, 8 * z : 8 * z + 8])
        put_edge(a_ref, c, -1, edge_ref[c])
        put_edge(a_ref, c, 8, beyond_ref[c])
    set_ghosts(a_ref)
    for z in range(PLANES):
        new = stepped(a_ref, z)
        for c in range(5):
            out_ref[c, z] = new[c] - mu * d_ref[c - 1, z] if c > 0 else new[c]
    misfit_ref[0] = jnp.sum(sums_ref[...]) * (1.0 / CELLS)


def f32(*shape):
    return jax.ShapeDtypeStruct(shape, jnp.float32)


VM = pl.BlockSpec(memory_space=pltpu.VMEM)
SM = pl.BlockSpec(memory_space=pltpu.SMEM)
PARAMS = pltpu.CompilerParams(vmem_limit_bytes=12 * 2**20)
BLOCK = (5, PLANES, 8, 128)
BLOCK4 = (4, PLANES, 8, 128)
FLAT = (5, PLANES * 8, 128)
FLAT4 = (4, PLANES * 8, 128)
EXTENDED = (5, (PLANES + 2) * PITCH, 128)


NEAR = [(i, i ^ 1) for i in range(TILES)]
FAR = [(i, (i + 1) % TILES if i % 2 else (i - 1) % TILES) for i in range(TILES)]


def shards(state, spacing_index, strength_index, obs_offsets):
    own = state.reshape(FLAT)

    def send(x, pairs):
        return lax.ppermute(x, "run", pairs)

    p = send(own, [(0, 8)])
    a, b, e = send(own, [(0, 2)]), send(own, [(0, 6)]), send(own, [(0, 4)])
    f, g, h = send(p, [(8, 10)]), send(p, [(8, 14)]), send(p, [(8, 12)])
    y = a + b + f + g
    u = send(y, [(2, 3), (6, 7), (10, 11), (14, 15)])
    v = send(y, [(2, 1), (6, 5), (10, 9), (14, 13)])

    nat, d, near, far = pl.pallas_call(
        pack_kernel,
        out_shape=(f32(*FLAT), f32(*FLAT4), f32(EDGES, 8, 128), f32(EDGES, 8, 128)),
        in_specs=[SM, SM] + [VM] * 7,
        out_specs=(VM,) * 4,
        compiler_params=PARAMS,
        name="pack",
    )(spacing_index, obs_offsets, own, y, u, v, p, e, h)

    near = lax.ppermute(near, "tile", NEAR)
    far = lax.ppermute(far, "tile", FAR)

    own1, nat1 = pl.pallas_call(
        inner_kernel,
        out_shape=(f32(*FLAT), f32(*FLAT)),
        in_specs=[SM] + [VM] * 3,
        out_specs=(VM,) * 2,
        scratch_shapes=[pltpu.VMEM(EXTENDED, jnp.float32)] * 2,
        compiler_params=PARAMS,
        name="inner",
    )(strength_index, own, nat, d)

    own2, beyond, edge, d2, sums = pl.pallas_call(
        steps_kernel,
        out_shape=(
            f32(*FLAT), f32(5, PLANES, 128), f32(5, PLANES, 128), f32(*BLOCK4), f32(TILES, 1, 128)
        ),
        in_specs=[SM, SM, SM] + [VM] * 7,
        out_specs=(VM,) * 5,
        scratch_shapes=[*[pltpu.VMEM(EXTENDED, jnp.float32)] * 2, pltpu.VMEM(ROWS, jnp.float32)],
        compiler_params=PARAMS,
        name="steps",
    )(spacing_index, strength_index, obs_offsets, own, nat, d, own1, nat1, near, far)

    edge = lax.ppermute(edge, "tile", [(i, (i + 1) % TILES) for i in range(TILES)])
    sums = lax.all_to_all(sums, "tile", 0, 0)

    out, misfit = pl.pallas_call(
        last_kernel,
        out_shape=(f32(*BLOCK), f32(1)),
        in_specs=[SM] + [VM] * 5,
        out_specs=(VM, SM),
        scratch_shapes=[pltpu.VMEM(EXTENDED, jnp.float32)],
        compiler_params=PARAMS,
        name="last",
    )(strength_index, own2, beyond, edge, d2, sums)
    return out[None], misfit


def solution(mesh):
    placed = (P("run", None, None, "tile", None), P("run"), P("run"), P())
    return jax.shard_map(
        shards,
        mesh=mesh,
        in_specs=placed,
        out_specs=(P("run", None, None, "tile", None), P("run")),
        check_vma=False,
    )
```

```python
import jax
import jax.numpy as jnp
from jax import lax
from jax.experimental import pallas as pl
from jax.experimental.pallas import tpu as pltpu
from jax.sharding import PartitionSpec as P

RUNS = 16
TILES = 32
PLANES = 8
CELLS = 8 * 256 * 128

DT = 0.05
VISC = 0.05
GAMMA1 = 0.4
GRAVITY = 0.5
HOT = 1.2
COLD = 0.8

ROWS = (8, 128)
UNROLL = 4


def rolled(v, shift, axis):
    return pltpu.roll(v, shift % v.shape[axis], axis)


def sub_ids():
    return lax.broadcasted_iota(jnp.int32, ROWS, 0)


def lane_ids():
    return lax.broadcasted_iota(jnp.int32, ROWS, 1)


class Spread:
    def __init__(self, sp_ref, off_ref):
        k = sp_ref[0]
        self.off = off_ref
        self.base = [lax.shift_left(lax.shift_right_logical(ids, k), k) for ids in (sub_ids(), lane_ids())]

    def plane(self, z):
        return self.base[0] + self.off[z, 0], self.base[1] + self.off[z, 1]

    def __call__(self, e, index):
        for axis in (0, 1):
            e = jnp.take_along_axis(e, index[axis], axis=axis, mode="promise_in_bounds")
        return e


PITCH = 24


def place(z, row):
    return (z + 1) * PITCH + 8 + row


def get(ref, c, z, shift=0):
    return ref[c, pl.ds(place(z, shift), 8)]


def put(ref, c, z, value):
    ref[c, pl.ds(pl.multiple_of(place(z, 0), 8), 8)] = value


def get_edge(ref, c, row):
    return ref[c, pl.ds(place(0, row), PLANES, stride=PITCH)]


def put_edge(ref, c, row, value):
    ref[c, pl.ds(place(0, row), PLANES, stride=PITCH)] = value


def mirrored(c, low, high):
    if c == 3:
        return -low, -high
    if c == 4:
        return 2.0 * HOT - low, 2.0 * COLD - high
    return low, high


def set_ghosts(ref):
    for c in range(5):
        low, high = mirrored(c, get(ref, c, 0), get(ref, c, PLANES - 1))
        put(ref, c, -1, low)
        put(ref, c, PLANES, high)


def advanced(c0, xn, xp, zn, zp):
    yn = [rolled(v, -1, 1) for v in c0]
    yp = [rolled(v, 1, 1) for v in c0]
    flux = (
        (xn[0] * xn[1] - xp[0] * xp[1])
        + (yn[0] * yn[2] - yp[0] * yp[2])
        + (zn[0] * zn[3] - zp[0] * zp[3])
    )
    scale = (0.5 * DT) / c0[0]
    grad = (
        xn[0] * xn[4] - xp[0] * xp[4],
        yn[0] * yn[4] - yp[0] * yp[4],
        zn[0] * zn[4] - zp[0] * zp[4],
    )
    new = [c0[0] - (0.5 * DT) * flux]
    div = None
    for q in range(1, 5):
        dx, dy, dz = xn[q] - xp[q], yn[q] - yp[q], zn[q] - zp[q]
        part = (None, dx, dy, dz, None)[q]
        if part is not None:
            div = part if div is None else div + part
        adv = c0[1] * dx + c0[2] * dy + c0[3] * dz
        six = ((xn[q] + xp[q]) + (yn[q] + yp[q])) + (zn[q] + zp[q])
        change = (DT * VISC) * (six - 6.0 * c0[q]) - (0.5 * DT) * adv
        if q < 4:
            change = change - grad[q - 1] * scale
            if q == 3:
                change = change - DT * GRAVITY
        else:
            change = change - (0.5 * DT * GAMMA1) * (c0[4] * div)
        new.append(c0[q] + change)
    return new


def stepped(ref, z):
    return advanced(
        *([get(ref, c, z + dz, dx) for c in range(5)] for dz, dx in ((0, 0), (0, 1), (0, -1), (1, 0), (-1, 0)))
    )


def edge_stepped(c0, xn, xp):
    sub = sub_ids()
    zn, zp = [], []
    for c in range(5):
        low, high = mirrored(c, c0[c], c0[c])
        zn.append(jnp.where(sub == PLANES - 1, high, rolled(c0[c], -1, 0)))
        zp.append(jnp.where(sub == 0, low, rolled(c0[c], 1, 0)))
    return advanced(c0, xn, xp, zn, zp)


def nudge_factor(st_ref):
    strength = 0.5 * lax.shift_left(jnp.int32(1), st_ref[0]).astype(jnp.float32)
    return jnp.where(lax.axis_index("run") == 0, 0.0, DT * strength)


EDGES = 30


def even_tile():
    return lax.rem(lax.axis_index("tile"), 2) == 0


def tile_of(z):
    return pl.ds(pl.multiple_of(8 * z, 8), 8)


def edge_of(ref, c, row):
    return ref[c, pl.ds(row, PLANES, stride=8)]


def planes(body):
    def several(i, carry):
        for k in range(UNROLL):
            body(i * UNROLL + k)
        return carry

    lax.fori_loop(0, PLANES // UNROLL, several, 0)


def pack_kernel(
    sp_ref, off_ref, own_ref, y_ref, u_ref, v_ref, w_ref, p_ref, nat_ref, d_ref, near_ref, far_ref
):
    spread = Spread(sp_ref, off_ref)
    even = even_tile()
    root = lax.axis_index("run") == 0
    for z in range(PLANES):
        index = spread.plane(z)
        here = pl.ds(8 * z, 8)
        for c in range(5):
            own = own_ref[c, here]
            nat = (y_ref[c, here] + u_ref[c, here]) + (v_ref[c, here] + w_ref[c, here]) + p_ref[c, here]
            nat = jnp.where(root, own, nat)
            nat_ref[c, here] = nat
            if c > 0:
                d_ref[c - 1, here] = spread(own - nat, index)
    fields = [(ref, c) for ref in (own_ref, nat_ref) for c in range(5)]
    left = [edge_of(ref, c, row) for ref, c in fields for row in (0, 1, 2)]
    right = [edge_of(ref, c, row) for ref, c in fields for row in (6, 7)] + [edge_of(d_ref, c, 7) for c in range(4)]
    for i in range(EDGES):
        to_right = right[min(i, len(right) - 1)]
        near_ref[i] = jnp.where(even, to_right, left[i])
        far_ref[i] = jnp.where(even, left[i], to_right)


def inner_kernel(st_ref, own_ref, nat_ref, d_ref, own1_ref, nat1_ref, a_ref, b_ref):
    mu = nudge_factor(st_ref)
    for ref, source in ((a_ref, own_ref), (b_ref, nat_ref)):
        for c in range(5):
            for z in range(PLANES):
                put(ref, c, z, source[c, 8 * z : 8 * z + 8])
        set_ghosts(ref)

    def first(z):
        new_a, new_b = stepped(a_ref, z), stepped(b_ref, z)
        for c in range(5):
            own1_ref[c, tile_of(z)] = new_a[c] - mu * d_ref[c - 1, tile_of(z)] if c > 0 else new_a[c]
            nat1_ref[c, tile_of(z)] = new_b[c]

    planes(first)


def steps_kernel(
    sp_ref, st_ref, off_ref, own_ref, nat_ref, d_ref, own1_ref, nat1_ref, far_ref, near_ref,
    own2_ref, beyond_ref, edge_ref, d2_ref, sum_ref, a1_ref, b1_ref, total_ref,
):
    spread = Spread(sp_ref, off_ref)
    even = even_tile()
    mu = nudge_factor(st_ref)
    sub = sub_ids()
    off_x, columns = jnp.zeros(ROWS, jnp.int32), spread.base[1]
    for z in range(PLANES):
        off_x = jnp.where(sub == z, off_ref[z, 0], off_x)
        columns = jnp.where(sub == z, spread.base[1] + off_ref[z, 1], columns)

    def observed(row8, row9):
        return jnp.take_along_axis(
            jnp.where(off_x == 0, row8, row9), columns, axis=1, mode="promise_in_bounds"
        )

    def sent(i, from_left):
        near, far = near_ref[i], far_ref[i]
        return jnp.where(even, far, near) if from_left else jnp.where(even, near, far)

    rows, next_rows = [], []
    for k, ref in ((0, own_ref), (1, nat_ref)):
        row = {
            j: [sent((5 * k + c) * width + i, j < 0) for c in range(5)]
            for j, width, i in ((-2, 2, 0), (-1, 2, 1), (8, 3, 0), (9, 3, 1), (10, 3, 2))
        }
        for j in (0, 1, 6, 7):
            row[j] = [edge_of(ref, c, j) for c in range(5)]
        rows.append(row)
        next_rows.append({j: edge_stepped(row[j], row[j + 1], row[j - 1]) for j in (-1, 0, 7, 8, 9)})
    for c in range(1, 5):
        d = observed(rows[0][8][c] - rows[1][8][c], rows[0][9][c] - rows[1][9][c])
        next_rows[0][-1][c] -= mu * sent(20 + c - 1, True)
        for j in (0, 7):
            next_rows[0][j][c] -= mu * edge_of(d_ref, c - 1, j)
        for j in (8, 9):
            next_rows[0][j][c] -= mu * d
    for ref, source, edge in ((a1_ref, own1_ref, next_rows[0]), (b1_ref, nat1_ref, next_rows[1])):
        for c in range(5):
            for z in range(PLANES):
                put(ref, c, z, source[c, 8 * z : 8 * z + 8])
            for j in (-1, 0, 7, 8):
                put_edge(ref, c, j, edge[j][c])
        set_ghosts(ref)

    def second(z):
        index = spread.plane(z)
        new_a, new_b = stepped(a1_ref, z), stepped(b1_ref, z)
        for c in range(5):
            value = new_a[c]
            if c > 0:
                value = value - mu * spread(get(a1_ref, c, z) - get(b1_ref, c, z), index)
                d = spread(value - new_b[c], index)
                d2_ref[c - 1, z] = d
                if c == 4:
                    total_ref[...] += d * d
            own2_ref[c, tile_of(z)] = value

    total_ref[...] = jnp.zeros(ROWS, jnp.float32)
    planes(second)
    own, nat = next_rows
    new = edge_stepped(own[8], own[9], own[7])
    for c in range(5):
        if c > 0:
            new[c] -= mu * observed(own[8][c] - nat[8][c], own[9][c] - nat[9][c])
        beyond_ref[c] = new[c]
        edge_ref[c] = edge_of(own2_ref, c, 7)
    total = jnp.sum(total_ref[...], axis=0)
    sum_ref[...] = jnp.broadcast_to(total[None, None], sum_ref.shape)


def last_kernel(st_ref, own_ref, beyond_ref, edge_ref, d_ref, sums_ref, out_ref, misfit_ref, a_ref):
    mu = nudge_factor(st_ref)
    for c in range(5):
        for z in range(PLANES):
            put(a_ref, c, z, own_ref[c, 8 * z : 8 * z + 8])
        put_edge(a_ref, c, -1, edge_ref[c])
        put_edge(a_ref, c, 8, beyond_ref[c])
    set_ghosts(a_ref)
    for z in range(PLANES):
        new = stepped(a_ref, z)
        for c in range(5):
            out_ref[c, z] = new[c] - mu * d_ref[c - 1, z] if c > 0 else new[c]
    misfit_ref[0] = jnp.sum(sums_ref[...]) * (1.0 / CELLS)


def f32(*shape):
    return jax.ShapeDtypeStruct(shape, jnp.float32)


VM = pl.BlockSpec(memory_space=pltpu.VMEM)
SM = pl.BlockSpec(memory_space=pltpu.SMEM)
PARAMS = pltpu.CompilerParams(vmem_limit_bytes=12 * 2**20)
BLOCK = (5, PLANES, 8, 128)
BLOCK4 = (4, PLANES, 8, 128)
FLAT = (5, PLANES * 8, 128)
FLAT4 = (4, PLANES * 8, 128)
EXTENDED = (5, (PLANES + 2) * PITCH, 128)


NEAR = [(i, i ^ 1) for i in range(TILES)]
FAR = [(i, (i + 1) % TILES if i % 2 else (i - 1) % TILES) for i in range(TILES)]


def shards(state, spacing_index, strength_index, obs_offsets):
    own = state.reshape(FLAT)

    def send(x, pairs):
        return lax.ppermute(x, "run", pairs)

    p = send(own, [(0, 8)])
    a, b = send(own, [(0, 2)]), send(own, [(0, 6)])
    f, g = send(p, [(8, 10)]), send(p, [(8, 14)])
    y = a + b + f + g
    u = send(y, [(2, 3), (6, 7), (10, 11), (14, 15)])
    v = send(y, [(2, 1), (6, 5), (10, 9), (14, 13)])
    w = send(y, [(2, 4), (10, 12)])

    nat, d, near, far = pl.pallas_call(
        pack_kernel,
        out_shape=(f32(*FLAT), f32(*FLAT4), f32(EDGES, 8, 128), f32(EDGES, 8, 128)),
        in_specs=[SM, SM] + [VM] * 6,
        out_specs=(VM,) * 4,
        compiler_params=PARAMS,
        name="pack",
    )(spacing_index, obs_offsets, own, y, u, v, w, p)

    near = lax.ppermute(near, "tile", NEAR)
    far = lax.ppermute(far, "tile", FAR)

    own1, nat1 = pl.pallas_call(
        inner_kernel,
        out_shape=(f32(*FLAT), f32(*FLAT)),
        in_specs=[SM] + [VM] * 3,
        out_specs=(VM,) * 2,
        scratch_shapes=[pltpu.VMEM(EXTENDED, jnp.float32)] * 2,
        compiler_params=PARAMS,
        name="inner",
    )(strength_index, own, nat, d)

    own2, beyond, edge, d2, sums = pl.pallas_call(
        steps_kernel,
        out_shape=(
            f32(*FLAT), f32(5, PLANES, 128), f32(5, PLANES, 128), f32(*BLOCK4), f32(TILES, 1, 128)
        ),
        in_specs=[SM, SM, SM] + [VM] * 7,
        out_specs=(VM,) * 5,
        scratch_shapes=[*[pltpu.VMEM(EXTENDED, jnp.float32)] * 2, pltpu.VMEM(ROWS, jnp.float32)],
        compiler_params=PARAMS,
        name="steps",
    )(spacing_index, strength_index, obs_offsets, own, nat, d, own1, nat1, far, near)

    edge = lax.ppermute(edge, "tile", [(i, (i + 1) % TILES) for i in range(TILES)])
    sums = lax.all_to_all(sums, "tile", 0, 0)

    out, misfit = pl.pallas_call(
        last_kernel,
        out_shape=(f32(*BLOCK), f32(1)),
        in_specs=[SM] + [VM] * 5,
        out_specs=(VM, SM),
        scratch_shapes=[pltpu.VMEM(EXTENDED, jnp.float32)],
        compiler_params=PARAMS,
        name="last",
    )(strength_index, own2, beyond, edge, d2, sums)
    return out[None], misfit


def solution(mesh):
    placed = (P("run", None, None, "tile", None), P("run"), P("run"), P())
    return jax.shard_map(
        shards,
        mesh=mesh,
        in_specs=placed,
        out_specs=(P("run", None, None, "tile", None), P("run")),
        check_vma=False,
    )
```

```python
import jax
import jax.numpy as jnp
from jax import lax
from jax.experimental import pallas as pl
from jax.experimental.pallas import tpu as pltpu
from jax.sharding import PartitionSpec as P

RUNS = 16
TILES = 32
PLANES = 8
CELLS = 8 * 256 * 128

DT = 0.05
VISC = 0.05
GAMMA1 = 0.4
GRAVITY = 0.5
HOT = 1.2
COLD = 0.8

ROWS = (8, 128)
UNROLL = 4


def rolled(v, shift, axis):
    return pltpu.roll(v, shift % v.shape[axis], axis)


def sub_ids():
    return lax.broadcasted_iota(jnp.int32, ROWS, 0)


def lane_ids():
    return lax.broadcasted_iota(jnp.int32, ROWS, 1)


class Spread:
    def __init__(self, sp_ref, off_ref):
        k = sp_ref[0]
        self.off = off_ref
        self.base = [lax.shift_left(lax.shift_right_logical(ids, k), k) for ids in (sub_ids(), lane_ids())]

    def plane(self, z):
        return self.base[0] + self.off[z, 0], self.base[1] + self.off[z, 1]

    def __call__(self, e, index):
        for axis in (0, 1):
            e = jnp.take_along_axis(e, index[axis], axis=axis, mode="promise_in_bounds")
        return e


PITCH = 24


def place(z, row):
    return (z + 1) * PITCH + 8 + row


def get(ref, c, z, shift=0):
    return ref[c, pl.ds(place(z, shift), 8)]


def put(ref, c, z, value):
    ref[c, pl.ds(pl.multiple_of(place(z, 0), 8), 8)] = value


def get_edge(ref, c, row):
    return ref[c, pl.ds(place(0, row), PLANES, stride=PITCH)]


def put_edge(ref, c, row, value):
    ref[c, pl.ds(place(0, row), PLANES, stride=PITCH)] = value


def mirrored(c, low, high):
    if c == 3:
        return -low, -high
    if c == 4:
        return 2.0 * HOT - low, 2.0 * COLD - high
    return low, high


def set_ghosts(ref):
    for c in range(5):
        low, high = mirrored(c, get(ref, c, 0), get(ref, c, PLANES - 1))
        put(ref, c, -1, low)
        put(ref, c, PLANES, high)


def advanced(c0, xn, xp, zn, zp):
    yn = [rolled(v, -1, 1) for v in c0]
    yp = [rolled(v, 1, 1) for v in c0]
    flux = (
        (xn[0] * xn[1] - xp[0] * xp[1])
        + (yn[0] * yn[2] - yp[0] * yp[2])
        + (zn[0] * zn[3] - zp[0] * zp[3])
    )
    scale = (0.5 * DT) / c0[0]
    grad = (
        xn[0] * xn[4] - xp[0] * xp[4],
        yn[0] * yn[4] - yp[0] * yp[4],
        zn[0] * zn[4] - zp[0] * zp[4],
    )
    new = [c0[0] - (0.5 * DT) * flux]
    div = None
    for q in range(1, 5):
        dx, dy, dz = xn[q] - xp[q], yn[q] - yp[q], zn[q] - zp[q]
        part = (None, dx, dy, dz, None)[q]
        if part is not None:
            div = part if div is None else div + part
        adv = c0[1] * dx + c0[2] * dy + c0[3] * dz
        six = ((xn[q] + xp[q]) + (yn[q] + yp[q])) + (zn[q] + zp[q])
        change = (DT * VISC) * (six - 6.0 * c0[q]) - (0.5 * DT) * adv
        if q < 4:
            change = change - grad[q - 1] * scale
            if q == 3:
                change = change - DT * GRAVITY
        else:
            change = change - (0.5 * DT * GAMMA1) * (c0[4] * div)
        new.append(c0[q] + change)
    return new


def stepped(ref, z):
    return advanced(
        *([get(ref, c, z + dz, dx) for c in range(5)] for dz, dx in ((0, 0), (0, 1), (0, -1), (1, 0), (-1, 0)))
    )


def edge_stepped(c0, xn, xp):
    sub = sub_ids()
    zn, zp = [], []
    for c in range(5):
        low, high = mirrored(c, c0[c], c0[c])
        zn.append(jnp.where(sub == PLANES - 1, high, rolled(c0[c], -1, 0)))
        zp.append(jnp.where(sub == 0, low, rolled(c0[c], 1, 0)))
    return advanced(c0, xn, xp, zn, zp)


def nudge_factor(st_ref):
    strength = 0.5 * lax.shift_left(jnp.int32(1), st_ref[0]).astype(jnp.float32)
    return jnp.where(lax.axis_index("run") == 0, 0.0, DT * strength)


EDGES = 30


def even_tile():
    return lax.rem(lax.axis_index("tile"), 2) == 0


def tile_of(z):
    return pl.ds(pl.multiple_of(8 * z, 8), 8)


def edge_of(ref, c, row):
    return ref[c, pl.ds(row, PLANES, stride=8)]


def planes(body):
    def several(i, carry):
        for k in range(UNROLL):
            body(i * UNROLL + k)
        return carry

    lax.fori_loop(0, PLANES // UNROLL, several, 0)


def pack_kernel(
    sp_ref, off_ref, own_ref, y_ref, u_ref, v_ref, w_ref, p_ref, nat_ref, d_ref, near_ref, far_ref
):
    spread = Spread(sp_ref, off_ref)
    even = even_tile()
    root = lax.axis_index("run") == 0
    for z in range(PLANES):
        index = spread.plane(z)
        here = pl.ds(8 * z, 8)
        for c in range(5):
            own = own_ref[c, here]
            nat = (y_ref[c, here] + u_ref[c, here]) + (v_ref[c, here] + w_ref[c, here]) + p_ref[c, here]
            nat = jnp.where(root, own, nat)
            nat_ref[c, here] = nat
            if c > 0:
                d_ref[c - 1, here] = spread(own - nat, index)
    fields = [(ref, c) for ref in (own_ref, nat_ref) for c in range(5)]
    left = [edge_of(ref, c, row) for ref, c in fields for row in (0, 1, 2)]
    right = [edge_of(ref, c, row) for ref, c in fields for row in (6, 7)] + [edge_of(d_ref, c, 7) for c in range(4)]
    for i in range(EDGES):
        to_right = right[min(i, len(right) - 1)]
        near_ref[i] = jnp.where(even, to_right, left[i])
        far_ref[i] = jnp.where(even, left[i], to_right)


def inner_kernel(st_ref, own_ref, nat_ref, d_ref, own1_ref, nat1_ref, a_ref, b_ref):
    mu = nudge_factor(st_ref)
    for ref, source in ((a_ref, own_ref), (b_ref, nat_ref)):
        for c in range(5):
            for z in range(PLANES):
                put(ref, c, z, source[c, 8 * z : 8 * z + 8])
        set_ghosts(ref)

    def first(z):
        new_a, new_b = stepped(a_ref, z), stepped(b_ref, z)
        for c in range(5):
            own1_ref[c, tile_of(z)] = new_a[c] - mu * d_ref[c - 1, tile_of(z)] if c > 0 else new_a[c]
            nat1_ref[c, tile_of(z)] = new_b[c]

    planes(first)


def steps_kernel(
    sp_ref, st_ref, off_ref, own_ref, nat_ref, d_ref, own1_ref, nat1_ref, far_ref, near_ref,
    own2_ref, beyond_ref, edge_ref, d2_ref, sum_ref, a1_ref, b1_ref, total_ref,
):
    spread = Spread(sp_ref, off_ref)
    even = even_tile()
    mu = nudge_factor(st_ref)
    sub = sub_ids()
    off_x, columns = jnp.zeros(ROWS, jnp.int32), spread.base[1]
    for z in range(PLANES):
        off_x = jnp.where(sub == z, off_ref[z, 0], off_x)
        columns = jnp.where(sub == z, spread.base[1] + off_ref[z, 1], columns)

    def observed(row8, row9):
        return jnp.take_along_axis(
            jnp.where(off_x == 0, row8, row9), columns, axis=1, mode="promise_in_bounds"
        )

    def sent(i, from_left):
        near, far = near_ref[i], far_ref[i]
        return jnp.where(even, far, near) if from_left else jnp.where(even, near, far)

    rows, next_rows = [], []
    for k, ref in ((0, own_ref), (1, nat_ref)):
        row = {
            j: [sent((5 * k + c) * width + i, j < 0) for c in range(5)]
            for j, width, i in ((-2, 2, 0), (-1, 2, 1), (8, 3, 0), (9, 3, 1), (10, 3, 2))
        }
        for j in (0, 1, 6, 7):
            row[j] = [edge_of(ref, c, j) for c in range(5)]
        rows.append(row)
        next_rows.append({j: edge_stepped(row[j], row[j + 1], row[j - 1]) for j in (-1, 0, 7, 8, 9)})
    for c in range(1, 5):
        d = observed(rows[0][8][c] - rows[1][8][c], rows[0][9][c] - rows[1][9][c])
        next_rows[0][-1][c] -= mu * sent(20 + c - 1, True)
        for j in (0, 7):
            next_rows[0][j][c] -= mu * edge_of(d_ref, c - 1, j)
        for j in (8, 9):
            next_rows[0][j][c] -= mu * d
    for ref, source, edge in ((a1_ref, own1_ref, next_rows[0]), (b1_ref, nat1_ref, next_rows[1])):
        for c in range(5):
            for z in range(PLANES):
                put(ref, c, z, source[c, 8 * z : 8 * z + 8])
            for j in (-1, 0, 7, 8):
                put_edge(ref, c, j, edge[j][c])
        set_ghosts(ref)

    def second(z):
        index = spread.plane(z)
        new_a, new_b = stepped(a1_ref, z), stepped(b1_ref, z)
        for c in range(5):
            value = new_a[c]
            if c > 0:
                value = value - mu * spread(get(a1_ref, c, z) - get(b1_ref, c, z), index)
                d = spread(value - new_b[c], index)
                d2_ref[c - 1, z] = d
                if c == 4:
                    total_ref[...] += d * d
            own2_ref[c, tile_of(z)] = value

    total_ref[...] = jnp.zeros(ROWS, jnp.float32)
    planes(second)
    own, nat = next_rows
    new = edge_stepped(own[8], own[9], own[7])
    for c in range(5):
        if c > 0:
            new[c] -= mu * observed(own[8][c] - nat[8][c], own[9][c] - nat[9][c])
        beyond_ref[c] = new[c]
        edge_ref[c] = edge_of(own2_ref, c, 7)
    total = jnp.sum(total_ref[...], axis=0)
    sum_ref[...] = jnp.broadcast_to(total[None], sum_ref.shape)


def last_kernel(st_ref, own_ref, beyond_ref, edge_ref, d_ref, sums_ref, out_ref, misfit_ref, a_ref):
    mu = nudge_factor(st_ref)
    for c in range(5):
        for z in range(PLANES):
            put(a_ref, c, z, own_ref[c, 8 * z : 8 * z + 8])
        put_edge(a_ref, c, -1, edge_ref[c])
        put_edge(a_ref, c, 8, beyond_ref[c])
    set_ghosts(a_ref)
    for z in range(PLANES):
        new = stepped(a_ref, z)
        for c in range(5):
            out_ref[c, z] = new[c] - mu * d_ref[c - 1, z] if c > 0 else new[c]
    misfit_ref[0] = jnp.sum(sums_ref[...]) * (1.0 / CELLS)


def f32(*shape):
    return jax.ShapeDtypeStruct(shape, jnp.float32)


VM = pl.BlockSpec(memory_space=pltpu.VMEM)
SM = pl.BlockSpec(memory_space=pltpu.SMEM)
PARAMS = pltpu.CompilerParams(vmem_limit_bytes=12 * 2**20)
BLOCK = (5, PLANES, 8, 128)
BLOCK4 = (4, PLANES, 8, 128)
FLAT = (5, PLANES * 8, 128)
FLAT4 = (4, PLANES * 8, 128)
EXTENDED = (5, (PLANES + 2) * PITCH, 128)


NEAR = [(i, i ^ 1) for i in range(TILES)]
FAR = [(i, (i + 1) % TILES if i % 2 else (i - 1) % TILES) for i in range(TILES)]


def shards(state, spacing_index, strength_index, obs_offsets):
    own = state.reshape(FLAT)

    def send(x, pairs):
        return lax.ppermute(x, "run", pairs)

    p = send(own, [(0, 8)])
    a, b = send(own, [(0, 2)]), send(own, [(0, 6)])
    f, g = send(p, [(8, 10)]), send(p, [(8, 14)])
    y = a + b + f + g
    u = send(y, [(2, 3), (6, 7), (10, 11), (14, 15)])
    v = send(y, [(2, 1), (6, 5), (10, 9), (14, 13)])
    w = send(y, [(2, 4), (10, 12)])

    nat, d, near, far = pl.pallas_call(
        pack_kernel,
        out_shape=(f32(*FLAT), f32(*FLAT4), f32(EDGES, 8, 128), f32(EDGES, 8, 128)),
        in_specs=[SM, SM] + [VM] * 6,
        out_specs=(VM,) * 4,
        compiler_params=PARAMS,
        name="pack",
    )(spacing_index, obs_offsets, own, y, u, v, w, p)

    near = lax.ppermute(near, "tile", NEAR)
    far = lax.ppermute(far, "tile", FAR)

    own1, nat1 = pl.pallas_call(
        inner_kernel,
        out_shape=(f32(*FLAT), f32(*FLAT)),
        in_specs=[SM] + [VM] * 3,
        out_specs=(VM,) * 2,
        scratch_shapes=[pltpu.VMEM(EXTENDED, jnp.float32)] * 2,
        compiler_params=PARAMS,
        name="inner",
    )(strength_index, own, nat, d)

    own2, beyond, edge, d2, sums = pl.pallas_call(
        steps_kernel,
        out_shape=(
            f32(*FLAT), f32(5, PLANES, 128), f32(5, PLANES, 128), f32(*BLOCK4), f32(TILES, 128)
        ),
        in_specs=[SM, SM, SM] + [VM] * 7,
        out_specs=(VM,) * 5,
        scratch_shapes=[*[pltpu.VMEM(EXTENDED, jnp.float32)] * 2, pltpu.VMEM(ROWS, jnp.float32)],
        compiler_params=PARAMS,
        name="steps",
    )(spacing_index, strength_index, obs_offsets, own, nat, d, own1, nat1, far, near)

    edge = lax.ppermute(edge, "tile", [(i, (i + 1) % TILES) for i in range(TILES)])
    sums = lax.all_to_all(sums, "tile", 0, 0, tiled=True)

    out, misfit = pl.pallas_call(
        last_kernel,
        out_shape=(f32(*BLOCK), f32(1)),
        in_specs=[SM] + [VM] * 5,
        out_specs=(VM, SM),
        scratch_shapes=[pltpu.VMEM(EXTENDED, jnp.float32)],
        compiler_params=PARAMS,
        name="last",
    )(strength_index, own2, beyond, edge, d2, sums)
    return out[None], misfit


def solution(mesh):
    placed = (P("run", None, None, "tile", None), P("run"), P("run"), P())
    return jax.shard_map(
        shards,
        mesh=mesh,
        in_specs=placed,
        out_specs=(P("run", None, None, "tile", None), P("run")),
        check_vma=False,
    )
```

```python
import jax
import jax.numpy as jnp
from jax import lax
from jax.experimental import pallas as pl
from jax.experimental.pallas import tpu as pltpu
from jax.sharding import PartitionSpec as P

RUNS = 16
TILES = 32
PLANES = 8
CELLS = 8 * 256 * 128

DT = 0.05
VISC = 0.05
GAMMA1 = 0.4
GRAVITY = 0.5
HOT = 1.2
COLD = 0.8

ROWS = (8, 128)
UNROLL = 4


def rolled(v, shift, axis):
    return pltpu.roll(v, shift % v.shape[axis], axis)


def sub_ids():
    return lax.broadcasted_iota(jnp.int32, ROWS, 0)


def lane_ids():
    return lax.broadcasted_iota(jnp.int32, ROWS, 1)


class Spread:
    def __init__(self, sp_ref, off_ref):
        k = sp_ref[0]
        self.off = off_ref
        self.base = [lax.shift_left(lax.shift_right_logical(ids, k), k) for ids in (sub_ids(), lane_ids())]

    def plane(self, z):
        return self.base[0] + self.off[z, 0], self.base[1] + self.off[z, 1]

    def __call__(self, e, index):
        for axis in (0, 1):
            e = jnp.take_along_axis(e, index[axis], axis=axis, mode="promise_in_bounds")
        return e


PITCH = 24


def place(z, row):
    return (z + 1) * PITCH + 8 + row


def get(ref, c, z, shift=0):
    return ref[c, pl.ds(place(z, shift), 8)]


def put(ref, c, z, value):
    ref[c, pl.ds(pl.multiple_of(place(z, 0), 8), 8)] = value


def get_edge(ref, c, row):
    return ref[c, pl.ds(place(0, row), PLANES, stride=PITCH)]


def put_edge(ref, c, row, value):
    ref[c, pl.ds(place(0, row), PLANES, stride=PITCH)] = value


def mirrored(c, low, high):
    if c == 3:
        return -low, -high
    if c == 4:
        return 2.0 * HOT - low, 2.0 * COLD - high
    return low, high


def set_ghosts(ref):
    for c in range(5):
        low, high = mirrored(c, get(ref, c, 0), get(ref, c, PLANES - 1))
        put(ref, c, -1, low)
        put(ref, c, PLANES, high)


def advanced(c0, xn, xp, zn, zp):
    yn = [rolled(v, -1, 1) for v in c0]
    yp = [rolled(v, 1, 1) for v in c0]
    flux = (
        (xn[0] * xn[1] - xp[0] * xp[1])
        + (yn[0] * yn[2] - yp[0] * yp[2])
        + (zn[0] * zn[3] - zp[0] * zp[3])
    )
    scale = (0.5 * DT) / c0[0]
    grad = (
        xn[0] * xn[4] - xp[0] * xp[4],
        yn[0] * yn[4] - yp[0] * yp[4],
        zn[0] * zn[4] - zp[0] * zp[4],
    )
    new = [c0[0] - (0.5 * DT) * flux]
    div = None
    for q in range(1, 5):
        dx, dy, dz = xn[q] - xp[q], yn[q] - yp[q], zn[q] - zp[q]
        part = (None, dx, dy, dz, None)[q]
        if part is not None:
            div = part if div is None else div + part
        adv = c0[1] * dx + c0[2] * dy + c0[3] * dz
        six = ((xn[q] + xp[q]) + (yn[q] + yp[q])) + (zn[q] + zp[q])
        change = (DT * VISC) * (six - 6.0 * c0[q]) - (0.5 * DT) * adv
        if q < 4:
            change = change - grad[q - 1] * scale
            if q == 3:
                change = change - DT * GRAVITY
        else:
            change = change - (0.5 * DT * GAMMA1) * (c0[4] * div)
        new.append(c0[q] + change)
    return new


def stepped(ref, z):
    return advanced(
        *([get(ref, c, z + dz, dx) for c in range(5)] for dz, dx in ((0, 0), (0, 1), (0, -1), (1, 0), (-1, 0)))
    )


def edge_stepped(c0, xn, xp):
    sub = sub_ids()
    zn, zp = [], []
    for c in range(5):
        low, high = mirrored(c, c0[c], c0[c])
        zn.append(jnp.where(sub == PLANES - 1, high, rolled(c0[c], -1, 0)))
        zp.append(jnp.where(sub == 0, low, rolled(c0[c], 1, 0)))
    return advanced(c0, xn, xp, zn, zp)


def nudge_factor(st_ref):
    strength = 0.5 * lax.shift_left(jnp.int32(1), st_ref[0]).astype(jnp.float32)
    return jnp.where(lax.axis_index("run") == 0, 0.0, DT * strength)


EDGES = 30


def even_tile():
    return lax.rem(lax.axis_index("tile"), 2) == 0


def tile_of(z):
    return pl.ds(pl.multiple_of(8 * z, 8), 8)


def edge_of(ref, c, row):
    return ref[c, pl.ds(row, PLANES, stride=8)]


def planes(body):
    def several(i, carry):
        for k in range(UNROLL):
            body(i * UNROLL + k)
        return carry

    lax.fori_loop(0, PLANES // UNROLL, several, 0)


def pack_kernel(
    sp_ref, off_ref, own_ref, y_ref, u_ref, v_ref, w_ref, p_ref, e_ref, nat_ref, d_ref, near_ref, far_ref
):
    spread = Spread(sp_ref, off_ref)
    even = even_tile()
    root = lax.axis_index("run") == 0
    for z in range(PLANES):
        index = spread.plane(z)
        here = pl.ds(8 * z, 8)
        for c in range(5):
            own = own_ref[c, here]
            nat = (y_ref[c, here] + u_ref[c, here]) + (v_ref[c, here] + w_ref[c, here]) + (p_ref[c, here] + e_ref[c, here])
            nat = jnp.where(root, own, nat)
            nat_ref[c, here] = nat
            if c > 0:
                d_ref[c - 1, here] = spread(own - nat, index)
    fields = [(ref, c) for ref in (own_ref, nat_ref) for c in range(5)]
    left = [edge_of(ref, c, row) for ref, c in fields for row in (0, 1, 2)]
    right = [edge_of(ref, c, row) for ref, c in fields for row in (6, 7)] + [edge_of(d_ref, c, 7) for c in range(4)]
    for i in range(EDGES):
        to_right = right[min(i, len(right) - 1)]
        near_ref[i] = jnp.where(even, to_right, left[i])
        far_ref[i] = jnp.where(even, left[i], to_right)


def inner_kernel(st_ref, own_ref, nat_ref, d_ref, own1_ref, nat1_ref, a_ref, b_ref):
    mu = nudge_factor(st_ref)
    for ref, source in ((a_ref, own_ref), (b_ref, nat_ref)):
        for c in range(5):
            for z in range(PLANES):
                put(ref, c, z, source[c, 8 * z : 8 * z + 8])
        set_ghosts(ref)

    def first(z):
        new_a, new_b = stepped(a_ref, z), stepped(b_ref, z)
        for c in range(5):
            own1_ref[c, tile_of(z)] = new_a[c] - mu * d_ref[c - 1, tile_of(z)] if c > 0 else new_a[c]
            nat1_ref[c, tile_of(z)] = new_b[c]

    planes(first)


def steps_kernel(
    sp_ref, st_ref, off_ref, own_ref, nat_ref, d_ref, own1_ref, nat1_ref, far_ref, near_ref,
    own2_ref, beyond_ref, edge_ref, d2_ref, sum_ref, a1_ref, b1_ref, total_ref,
):
    spread = Spread(sp_ref, off_ref)
    even = even_tile()
    mu = nudge_factor(st_ref)
    sub = sub_ids()
    off_x, columns = jnp.zeros(ROWS, jnp.int32), spread.base[1]
    for z in range(PLANES):
        off_x = jnp.where(sub == z, off_ref[z, 0], off_x)
        columns = jnp.where(sub == z, spread.base[1] + off_ref[z, 1], columns)

    def observed(row8, row9):
        return jnp.take_along_axis(
            jnp.where(off_x == 0, row8, row9), columns, axis=1, mode="promise_in_bounds"
        )

    def sent(i, from_left):
        near, far = near_ref[i], far_ref[i]
        return jnp.where(even, far, near) if from_left else jnp.where(even, near, far)

    rows, next_rows = [], []
    for k, ref in ((0, own_ref), (1, nat_ref)):
        row = {
            j: [sent((5 * k + c) * width + i, j < 0) for c in range(5)]
            for j, width, i in ((-2, 2, 0), (-1, 2, 1), (8, 3, 0), (9, 3, 1), (10, 3, 2))
        }
        for j in (0, 1, 6, 7):
            row[j] = [edge_of(ref, c, j) for c in range(5)]
        rows.append(row)
        next_rows.append({j: edge_stepped(row[j], row[j + 1], row[j - 1]) for j in (-1, 0, 7, 8, 9)})
    for c in range(1, 5):
        d = observed(rows[0][8][c] - rows[1][8][c], rows[0][9][c] - rows[1][9][c])
        next_rows[0][-1][c] -= mu * sent(20 + c - 1, True)
        for j in (0, 7):
            next_rows[0][j][c] -= mu * edge_of(d_ref, c - 1, j)
        for j in (8, 9):
            next_rows[0][j][c] -= mu * d
    for ref, source, edge in ((a1_ref, own1_ref, next_rows[0]), (b1_ref, nat1_ref, next_rows[1])):
        for c in range(5):
            for z in range(PLANES):
                put(ref, c, z, source[c, 8 * z : 8 * z + 8])
            for j in (-1, 0, 7, 8):
                put_edge(ref, c, j, edge[j][c])
        set_ghosts(ref)

    def second(z):
        index = spread.plane(z)
        new_a, new_b = stepped(a1_ref, z), stepped(b1_ref, z)
        for c in range(5):
            value = new_a[c]
            if c > 0:
                value = value - mu * spread(get(a1_ref, c, z) - get(b1_ref, c, z), index)
                d = spread(value - new_b[c], index)
                d2_ref[c - 1, z] = d
                if c == 4:
                    total_ref[...] += d * d
            own2_ref[c, tile_of(z)] = value

    total_ref[...] = jnp.zeros(ROWS, jnp.float32)
    planes(second)
    own, nat = next_rows
    new = edge_stepped(own[8], own[9], own[7])
    for c in range(5):
        if c > 0:
            new[c] -= mu * observed(own[8][c] - nat[8][c], own[9][c] - nat[9][c])
        beyond_ref[c] = new[c]
        edge_ref[c] = edge_of(own2_ref, c, 7)
    total = jnp.sum(total_ref[...], axis=0)
    sum_ref[...] = jnp.broadcast_to(total[None], sum_ref.shape)


def last_kernel(st_ref, own_ref, beyond_ref, edge_ref, d_ref, sums_ref, out_ref, misfit_ref, a_ref):
    mu = nudge_factor(st_ref)
    for c in range(5):
        for z in range(PLANES):
            put(a_ref, c, z, own_ref[c, 8 * z : 8 * z + 8])
        put_edge(a_ref, c, -1, edge_ref[c])
        put_edge(a_ref, c, 8, beyond_ref[c])
    set_ghosts(a_ref)
    for z in range(PLANES):
        new = stepped(a_ref, z)
        for c in range(5):
            out_ref[c, z] = new[c] - mu * d_ref[c - 1, z] if c > 0 else new[c]
    misfit_ref[0] = jnp.sum(sums_ref[...]) * (1.0 / CELLS)


def f32(*shape):
    return jax.ShapeDtypeStruct(shape, jnp.float32)


VM = pl.BlockSpec(memory_space=pltpu.VMEM)
SM = pl.BlockSpec(memory_space=pltpu.SMEM)
PARAMS = pltpu.CompilerParams(vmem_limit_bytes=12 * 2**20)
BLOCK = (5, PLANES, 8, 128)
BLOCK4 = (4, PLANES, 8, 128)
FLAT = (5, PLANES * 8, 128)
FLAT4 = (4, PLANES * 8, 128)
EXTENDED = (5, (PLANES + 2) * PITCH, 128)


NEAR = [(i, i ^ 1) for i in range(TILES)]
FAR = [(i, (i + 1) % TILES if i % 2 else (i - 1) % TILES) for i in range(TILES)]


def shards(state, spacing_index, strength_index, obs_offsets):
    own = state.reshape(FLAT)

    def send(x, pairs):
        return lax.ppermute(x, "run", pairs)

    p = send(own, [(0, 8)])
    a, b, e = send(own, [(0, 2)]), send(own, [(0, 6)]), send(own, [(0, 4)])
    f, g = send(p, [(8, 10)]), send(p, [(8, 14)])
    y = a + b + f + g
    u = send(y, [(2, 3), (6, 7), (10, 11), (14, 15)])
    v = send(y, [(2, 1), (6, 5), (10, 9), (14, 13)])
    w = send(y, [(10, 12)])

    nat, d, near, far = pl.pallas_call(
        pack_kernel,
        out_shape=(f32(*FLAT), f32(*FLAT4), f32(EDGES, 8, 128), f32(EDGES, 8, 128)),
        in_specs=[SM, SM] + [VM] * 7,
        out_specs=(VM,) * 4,
        compiler_params=PARAMS,
        name="pack",
    )(spacing_index, obs_offsets, own, y, u, v, w, p, e)

    near = lax.ppermute(near, "tile", NEAR)
    far = lax.ppermute(far, "tile", FAR)

    own1, nat1 = pl.pallas_call(
        inner_kernel,
        out_shape=(f32(*FLAT), f32(*FLAT)),
        in_specs=[SM] + [VM] * 3,
        out_specs=(VM,) * 2,
        scratch_shapes=[pltpu.VMEM(EXTENDED, jnp.float32)] * 2,
        compiler_params=PARAMS,
        name="inner",
    )(strength_index, own, nat, d)

    own2, beyond, edge, d2, sums = pl.pallas_call(
        steps_kernel,
        out_shape=(
            f32(*FLAT), f32(5, PLANES, 128), f32(5, PLANES, 128), f32(*BLOCK4), f32(TILES, 128)
        ),
        in_specs=[SM, SM, SM] + [VM] * 7,
        out_specs=(VM,) * 5,
        scratch_shapes=[*[pltpu.VMEM(EXTENDED, jnp.float32)] * 2, pltpu.VMEM(ROWS, jnp.float32)],
        compiler_params=PARAMS,
        name="steps",
    )(spacing_index, strength_index, obs_offsets, own, nat, d, own1, nat1, far, near)

    edge = lax.ppermute(edge, "tile", [(i, (i + 1) % TILES) for i in range(TILES)])
    sums = lax.all_to_all(sums, "tile", 0, 0, tiled=True)

    out, misfit = pl.pallas_call(
        last_kernel,
        out_shape=(f32(*BLOCK), f32(1)),
        in_specs=[SM] + [VM] * 5,
        out_specs=(VM, SM),
        scratch_shapes=[pltpu.VMEM(EXTENDED, jnp.float32)],
        compiler_params=PARAMS,
        name="last",
    )(strength_index, own2, beyond, edge, d2, sums)
    return out[None], misfit


def solution(mesh):
    placed = (P("run", None, None, "tile", None), P("run"), P("run"), P())
    return jax.shard_map(
        shards,
        mesh=mesh,
        in_specs=placed,
        out_specs=(P("run", None, None, "tile", None), P("run")),
        check_vma=False,
    )
```
